32 devices in a mesh: sec: 4 (over x, core), dp: 4 (over z), tp: 2 (over y).
Axes of the slice: x: 2, y: 2, z: 4, core: 2. Of those that a mesh axis runs over, the one named last changes fastest.
Arguments:
- responses: bfloat16 [16, 128, 8192], P(('sec', 'dp'), 'tp'), may hold values from -6 to 6
- lengths: int32 [16], replicated, may hold values from 1 to 128, 1280 in all
- dest_dp: int32 [4, 16], replicated, may hold values from 0 to 3, as said below
- dest_slot: int32 [4, 16], replicated, may hold values from 0 to 5, as said below
- wq: bfloat16 [4, 8192, 4096], P('sec', None, 'tp'), may hold values from -0.0625 to 0.0625
- wkv: bfloat16 [4, 2, 8192, 1024], P('sec', None, None, 'tp'), may hold values from -0.0625 to 0.0625
- wo: bfloat16 [4, 4096, 8192], P('sec', 'tp'), may hold values from -0.09375 to 0.09375
- norm_gain: float32 [4, 8192], P('sec')
- head_vec: float32 [4, 8192], P('sec'), may hold values from -0.0625 to 0.0625
Outputs:
- layer_out: bfloat16 [4, 4, 128, 6, 8192], P('sec', 'dp', 'tp')
- sample_scores: float32 [4, 6, 4], P('dp')
The draws below stay inside these ranges and needn't reach their ends.
Inputs may be any that keep to these rules, and one draw needn't show every extreme that they name: `dest_dp`: in each model's row, the responses go to the 4 groups; no group receives more than 6 responses and one group of every model receives exactly 6. `dest_slot`: within one model and one group, the responses take distinct rows; a group that receives c responses uses rows 0 to c - 1.
All inputs are finite; a program needn't handle non-finite values.
Results may differ from the reference program's by a relative error of at most 0.018.
The reference program's roundings to bfloat16 on the way count: a program that leaves them out, or rounds other values in their place, can miss the bound.
Values may be sent and summed in bfloat16 or wider, within the bound.
No kernel may reach another device: no remote copies, remote signals or barrier semaphores. Data moves between devices by JAX's collectives and lax.ppermute only.
A program may use at most 256 MiB of HBM per device.

```python
import math
import jax
import jax.numpy as jnp
import numpy as np
from jax import lax

D = 8192
QH = 32
KVH = 8
HD = 128
MAXLEN = 128
SAMPLES = 16
SLOTS = 6
N_SEC = 4
N_DP = 4
N_TP = 2


def packing(base_key):
    section_keys = jax.random.split(jax.random.fold_in(base_key, 101), N_SEC)

    def draw_section(subkey):
        shuffled = jax.random.permutation(jax.random.fold_in(subkey, 1), SAMPLES)
        first_group = jax.random.randint(jax.random.fold_in(subkey, 2), (), 0, N_DP)
        position_rank = jnp.arange(SAMPLES)
        remainder = jnp.maximum(position_rank - SLOTS, 0)
        group_table = jnp.where(position_rank < SLOTS, first_group, (first_group + 1 + remainder % (N_DP - 1)) % N_DP)
        row_number = jnp.where(position_rank < SLOTS, position_rank, remainder // (N_DP - 1))
        destination = jnp.zeros((SAMPLES,), jnp.int32).at[shuffled].set(group_table.astype(jnp.int32))
        row_table = jnp.zeros((SAMPLES,), jnp.int32).at[shuffled].set(row_number.astype(jnp.int32))
        return (destination, row_table)
    return jax.vmap(draw_section)(section_keys)


def draw_dest_dp(key, part):
    return packing(key)[0]


def draw_dest_slot(key, part):
    return packing(key)[1]


def draw_norm_gain(key, part):
    gains = jax.random.uniform(key, (N_SEC, D), jnp.float32, 0.6, 1.6)
    return gains.astype(jnp.float32)


def block_levels(own_key, shape, cuts, least, top_value):
    loudness, own = 1.0, jax.random.fold_in(own_key, 6)
    for position, blocks in cuts:
        steps = jnp.exp(jax.random.uniform(jax.random.fold_in(own, position), (blocks,), jnp.float32, least / len(cuts), top_value / len(cuts)))
        loudness = loudness * jnp.repeat(steps, shape[position] // blocks).reshape([-1 if axis == position else 1 for axis in range(len(shape))])
    return loudness


def split_up(amount, total, limit, lean):
    weights = [(1 << 20) // math.isqrt(rank ** lean) + 1 for rank in range(2, amount + 1)]
    rest, counts = total - limit - (amount - 1), [1] * (amount - 1)
    while rest > 0:
        movable = [i for i in range(amount - 1) if counts[i] < limit]
        mass, left = sum([weights[i] for i in movable]), rest
        for i in movable:
            extra = min(limit - counts[i], max(1, left * weights[i] // mass), rest)
            counts[i] = counts[i] + extra
            rest = rest - extra
    return np.array([limit] + counts)


def uneven_parts(key, count, total, limit, skew):
    if count == 2:
        one = jax.random.randint(key, (), max(1, total - limit), min(limit, total - 1) + 1)
        return jnp.stack([one, total - one])
    sizes = jnp.asarray(split_up(count, total, limit, skew), jnp.int32)
    twos = (count - 1) // 2
    source_of, receiver = sizes[1:1 + 2 * twos:2], sizes[2:2 + 2 * twos:2]
    margin = jnp.minimum(source_of - 1, limit - receiver)
    passed = jax.random.randint(jax.random.fold_in(key, 1), (twos,), 0, 1 << 20) % (margin + 1)
    sizes = sizes.at[1:1 + 2 * twos:2].set(source_of - passed).at[2:2 + 2 * twos:2].set(receiver + passed)
    return sizes[jax.random.permutation(jax.random.fold_in(key, 2), count)]


def noise(key, shape, spread, most, pieces=(), kind=jnp.bfloat16):
    array = jax.random.normal(key, shape, jnp.float32) * spread
    if len(pieces) > 0:
        array = block_levels(key, shape, pieces, -0.22, 0.18) * array
    return jnp.clip(array, min=-most, max=most).astype(kind)


def setup_inputs(seed: int = 0) -> dict:
    streams_of = jax.random.split(jax.random.key(seed), 10)
    return {
        "responses": noise(streams_of[0], (SAMPLES, MAXLEN, D), 1.0, 6.0, ((0, 16), (1, 2))),
        "lengths": uneven_parts(streams_of[1], SAMPLES, SAMPLES * MAXLEN * 5 // 8, MAXLEN, 2).astype(jnp.int32),
        "dest_dp": draw_dest_dp(jax.random.fold_in(streams_of[9], 71), 0),
        "dest_slot": draw_dest_slot(jax.random.fold_in(streams_of[9], 71), 0),
        "wq": noise(streams_of[4], (N_SEC, D, QH * HD), D ** -0.5, 0.0625, ((0, 4), (2, 2))),
        "wkv": noise(streams_of[5], (N_SEC, 2, D, KVH * HD), D ** -0.5, 0.0625, ((0, 4), (3, 2))),
        "wo": noise(streams_of[6], (N_SEC, QH * HD, D), (QH * HD) ** -0.5, 0.09375, ((0, 4), (1, 2))),
        "norm_gain": draw_norm_gain(jax.random.fold_in(streams_of[9], 71), 0),
        "head_vec": noise(streams_of[8], (N_SEC, D), D ** -0.5, 0.0625, ((0, 4),), jnp.float32),
    }


norm_eps = 1e-05
rope_theta = 500000.0

def rope_tables(positions, full_width):
    half_width = full_width // 2
    frequency = jnp.exp(jnp.arange(half_width, dtype=jnp.float32) * (-2.0 * math.log(rope_theta) / full_width))
    angles = positions.astype(jnp.float32)[:, None] * frequency[None, :]
    return (jnp.cos(angles), jnp.sin(angles))

def rotate(values_in, cosine_table, sine_table):
    half_width = values_in.shape[-1] // 2
    first_half = values_in[..., :half_width]
    second_half = values_in[..., half_width:]
    return jnp.concatenate([first_half * cosine_table - second_half * sine_table, second_half * cosine_table + first_half * sine_table], axis=-1)

def attention_layer(rows, w_query, w_key, w_value, w_out, scale_vec, head_vector):
    seq_len = rows.shape[0]
    positions = jnp.arange(seq_len)
    as_float = rows.astype(jnp.float32)
    normed = (as_float * lax.rsqrt(lax.optimization_barrier(jnp.mean(as_float * as_float, axis=-1, keepdims=True)) + norm_eps) * scale_vec).astype(jnp.bfloat16)
    cosine_table, sine_table = rope_tables(positions, HD)
    cosine_table = cosine_table[:, None, :]
    sine_table = sine_table[:, None, :]
    queries = jnp.dot(normed, w_query, preferred_element_type=jnp.float32).reshape(seq_len, QH, HD)
    queries = rotate(queries, cosine_table, sine_table).astype(jnp.bfloat16)
    keys_rot = jnp.dot(normed, w_key, preferred_element_type=jnp.float32).reshape(seq_len, KVH, HD)
    keys_rot = rotate(keys_rot, cosine_table, sine_table).astype(jnp.bfloat16)
    values = jnp.dot(normed, w_value, preferred_element_type=jnp.float32).astype(jnp.bfloat16).reshape(seq_len, KVH, HD)
    grouped = queries.reshape(seq_len, KVH, QH // KVH, HD)
    scores = jnp.einsum('ikgh,jkh->kgij', grouped.astype(jnp.float32), keys_rot.astype(jnp.float32)) / math.sqrt(HD)
    causal = positions[:, None] >= positions[None, :]
    scores = jnp.where(causal, scores, -1e+30)
    peak = lax.optimization_barrier(jnp.max(scores, axis=-1, keepdims=True))
    expo = jnp.exp(scores - peak)
    attention_weights = (expo / lax.optimization_barrier(jnp.sum(expo, axis=-1, keepdims=True))).astype(jnp.bfloat16)
    context = jnp.einsum('kgij,jkh->ikgh', attention_weights.astype(jnp.float32), values.astype(jnp.float32))
    context = context.astype(jnp.bfloat16).reshape(seq_len, QH * HD)
    per_team = jnp.einsum('ltf,tfd->tld', context.reshape(seq_len, N_TP, QH * HD // N_TP).astype(jnp.float32), w_out.reshape(N_TP, QH * HD // N_TP, D).astype(jnp.float32))
    per_team = lax.optimization_barrier(per_team.astype(jnp.bfloat16)).astype(jnp.float32)
    hidden = as_float + lax.optimization_barrier(jnp.sum(per_team, axis=0))
    token_scores = lax.optimization_barrier(jnp.sum(hidden * lax.rsqrt(lax.optimization_barrier(jnp.mean(hidden * hidden, axis=-1, keepdims=True)) + norm_eps) * head_vector, axis=-1))
    return (hidden, token_scores)

def reference(responses, lengths, dest_dp, dest_slot, wq, wkv, wo, norm_gain, head_vec):
    positions = jnp.arange(MAXLEN)
    is_valid = positions[None, :] < lengths[:, None]
    rows_out = jnp.zeros((N_SEC, N_DP, MAXLEN, SLOTS, D), jnp.bfloat16)
    sums_list = []
    for section in range(N_SEC):

        def per_sample(sample_rows):
            return attention_layer(sample_rows, wq[section], wkv[section, 0], wkv[section, 1], wo[section], norm_gain[section], head_vec[section])
        hidden, token_scores = lax.map(per_sample, responses)
        masked = jnp.where(is_valid[:, :, None], hidden, 0.0).astype(jnp.bfloat16)
        rows_out = rows_out.at[section, dest_dp[section], :, dest_slot[section]].set(masked)
        sums_list.append(lax.optimization_barrier(jnp.sum(jnp.where(is_valid, token_scores, 0.0), axis=1)))
    averages = jnp.stack(sums_list, axis=0) / lengths[None, :].astype(jnp.float32)
    sample_scores = jnp.zeros((N_DP, SLOTS, N_SEC), jnp.float32).at[dest_dp[N_SEC - 1], dest_slot[N_SEC - 1]].set(averages.T)
    return (rows_out, sample_scores)
```

```python
import functools
import math

import jax
import jax.numpy as jnp
from jax import lax
from jax.experimental import pallas as pl
from jax.experimental.pallas import tpu as pltpu
from jax.sharding import PartitionSpec as P

HD = 128
NORM_EPS = 1e-05
ROPE_THETA = 500000.0
VMEM_BYTES = 56 * 1024 * 1024
N_CHUNKS = 8


def params():
    return pltpu.CompilerParams(vmem_limit_bytes=VMEM_BYTES)


def swap(value, axis, size, step):
    return lax.ppermute(value, axis, [(j, j ^ step) for j in range(size)])


def shift(value, axis, size, step):
    return lax.ppermute(value, axis, [(j, (j + step) % size) for j in range(size)])


def attention_kernel(n_dp, n_tp, x_ref, gain_ref, cos_ref, sin_ref, mask_ref, wq_ref, wkv_ref, out_ref, normed, acc_q, acc_k, acc_v):
    group, step = pl.program_id(0), pl.program_id(1)
    steps, rows, depth = normed.shape
    seq = mask_ref.shape[0]
    width = steps * depth

    @pl.when((group == 0) & (step == 0))
    def _():
        def norm_rows(i, carry):
            at = pl.ds(pl.multiple_of(i * 16, 16), 16)
            x = x_ref[at, :].astype(jnp.float32)
            inv = lax.rsqrt(jnp.sum(x * x, axis=-1, keepdims=True) * (1.0 / width) + NORM_EPS)
            y = (x * inv * gain_ref[...]).astype(jnp.bfloat16)
            for j in range(steps):
                normed[j, at, :] = y[:, j * depth : (j + 1) * depth]
            return carry

        lax.fori_loop(0, rows // 16, norm_rows, 0)

    lhs = normed[step]
    part_q = jnp.dot(lhs, wq_ref[...], preferred_element_type=jnp.float32)
    part_k = jnp.dot(lhs, wkv_ref[0], preferred_element_type=jnp.float32)
    part_v = jnp.dot(lhs, wkv_ref[1], preferred_element_type=jnp.float32)

    @pl.when(step == 0)
    def _():
        acc_q[...] = part_q
        acc_k[...] = part_k
        acc_v[...] = part_v

    @pl.when(step > 0)
    def _():
        acc_q[...] += part_q
        acc_k[...] += part_k
        acc_v[...] += part_v

    @pl.when(step == steps - 1)
    def _():
        cos, sin = cos_ref[...], sin_ref[...]
        causal = mask_ref[...] > 0.0
        block = seq // (n_dp * n_tp)
        kv_here = acc_k.shape[1] // HD
        per_kv = acc_q.shape[1] // acc_k.shape[1]

        def rope(v):
            return (v * cos + pltpu.roll(v, HD // 2, 1) * sin).astype(jnp.bfloat16)

        for s in range(rows // seq):
            at = slice(s * seq, (s + 1) * seq)
            for j in range(kv_here):
                cols = slice(j * HD, (j + 1) * HD)
                keys = rope(acc_k[at, cols])
                values = acc_v[at, cols].astype(jnp.bfloat16)
                for h in range(per_kv):
                    head = j * per_kv + h
                    hcols = slice(head * HD, (head + 1) * HD)
                    queries = rope(acc_q[at, hcols])
                    scores = lax.dot_general(
                        queries, keys, (((1,), (1,)), ((), ())), preferred_element_type=jnp.float32
                    ) * (1.0 / math.sqrt(HD))
                    scores = jnp.where(causal, scores, -1e30)
                    expo = jnp.exp(scores - jnp.max(scores, axis=-1, keepdims=True))
                    weights = (expo / jnp.sum(expo, axis=-1, keepdims=True)).astype(jnp.bfloat16)
                    context = jnp.dot(weights, values, preferred_element_type=jnp.float32).astype(jnp.bfloat16)
                    for t in range(n_tp):
                        for z in range(n_dp):
                            start = (t * n_dp + z) * block
                            out_ref[z, t, s, :, hcols] = context[start : start + block]


def attention(rows_in, gain, cos, sin, mask, wq, wkv, n_dp, n_tp):
    rows, width = rows_in.shape
    seq = mask.shape[0]
    q_width, kv_width = wq.shape[2], wkv.shape[3]
    kv_block = min(2 * HD, kv_width)
    groups = kv_width // kv_block
    q_block = q_width // groups
    steps = 4
    depth = width // steps
    samples = rows // seq
    block = seq // (n_dp * n_tp)
    fixed = lambda g, k: (0, 0)
    return pl.pallas_call(
        functools.partial(attention_kernel, n_dp, n_tp),
        out_shape=jax.ShapeDtypeStruct((n_dp, n_tp, samples, block, q_width), jnp.bfloat16),
        grid=(groups, steps),
        in_specs=[
            pl.BlockSpec((rows, width), fixed),
            pl.BlockSpec((1, width), fixed),
            pl.BlockSpec((seq, HD), fixed),
            pl.BlockSpec((seq, HD), fixed),
            pl.BlockSpec((seq, seq), fixed),
            pl.BlockSpec((None, depth, q_block), lambda g, k: (0, k, g)),
            pl.BlockSpec((None, 2, depth, kv_block), lambda g, k: (0, 0, k, g)),
        ],
        out_specs=pl.BlockSpec((n_dp, n_tp, samples, block, q_block), lambda g, k: (0, 0, 0, 0, g)),
        scratch_shapes=[
            pltpu.VMEM((steps, rows, depth), jnp.bfloat16),
            pltpu.VMEM((rows, q_block), jnp.float32),
            pltpu.VMEM((rows, kv_block), jnp.float32),
            pltpu.VMEM((rows, kv_block), jnp.float32),
        ],
        compiler_params=params(),
        cost_estimate=pl.CostEstimate(
            flops=2 * rows * width * (q_width + 2 * kv_width),
            bytes_accessed=2 * width * (q_width + 2 * kv_width) + 4 * rows * width,
            transcendentals=0,
        ),
        name="project_and_attend",
    )(rows_in, gain, cos, sin, mask, wq, wkv)


def out_kernel(ctx_ref, wo_ref, own_ref, send_ref):
    full = jnp.dot(ctx_ref[...], wo_ref[...], preferred_element_type=jnp.float32).astype(jnp.bfloat16)
    mine = own_ref.shape[0]
    own_ref[...] = full[:mine]
    send_ref[...] = full[mine:]


def out_projection(ctx, wo, mine, chunk, cols):
    rows, depth = ctx.shape
    col_block = min(512, cols)
    inner = cols // col_block
    return pl.pallas_call(
        out_kernel,
        out_shape=[
            jax.ShapeDtypeStruct((mine, cols), jnp.bfloat16),
            jax.ShapeDtypeStruct((rows - mine, cols), jnp.bfloat16),
        ],
        grid=(inner,),
        in_specs=[
            pl.BlockSpec((rows, depth), lambda n: (0, 0)),
            pl.BlockSpec((None, depth, col_block), lambda n: (0, 0, chunk * inner + n)),
        ],
        out_specs=[
            pl.BlockSpec((mine, col_block), lambda n: (0, n)),
            pl.BlockSpec((rows - mine, col_block), lambda n: (0, n)),
        ],
        compiler_params=params(),
        cost_estimate=pl.CostEstimate(
            flops=2 * rows * depth * cols,
            bytes_accessed=2 * depth * cols + 2 * rows * (depth + cols),
            transcendentals=0,
        ),
        name="out_projection",
    )(ctx, wo)


def join_kernel(n_slots, block, table_ref, own_ref, other_ref, resid_ref, head_ref, packed_ref, stats_ref):
    dest = pl.program_id(0)
    head = head_ref[...]
    lane = lax.broadcasted_iota(jnp.int32, (block, HD), 1)
    row = lax.broadcasted_iota(jnp.int32, (block, 1), 0)

    def one_slot(slot, carry):
        entry = dest * n_slots + slot
        part, resid, live = table_ref[0, entry], table_ref[1, entry], table_ref[2, entry]
        added = own_ref[part].astype(jnp.float32)
        for k in range(other_ref.shape[0]):
            added = added + other_ref[k, part].astype(jnp.float32)
        hidden = resid_ref[resid].astype(jnp.float32) + added
        packed_ref[slot] = jnp.where(row < live, hidden, 0.0).astype(jnp.bfloat16)
        squares = jnp.sum(hidden * hidden, axis=-1, keepdims=True)
        scored = jnp.sum(hidden * head, axis=-1, keepdims=True)
        stats_ref[slot] = jnp.where(lane == 0, squares, jnp.where(lane == 1, scored, 0.0))
        return carry

    lax.fori_loop(0, n_slots, one_slot, 0)


def join(table, own, other, resid, head, chunk, n_dp, n_slots, block):
    blocks, _, cols = own.shape
    return pl.pallas_call(
        functools.partial(join_kernel, n_slots, block),
        out_shape=[
            jax.ShapeDtypeStruct((n_dp, n_slots, block, cols), jnp.bfloat16),
            jax.ShapeDtypeStruct((n_dp, n_slots, block, HD), jnp.float32),
        ],
        grid_spec=pltpu.PrefetchScalarGridSpec(
            num_scalar_prefetch=1,
            grid=(n_dp,),
            in_specs=[
                pl.BlockSpec(own.shape, lambda d, t: (0, 0, 0)),
                pl.BlockSpec(other.shape, lambda d, t: (0, 0, 0, 0)),
                pl.BlockSpec((blocks, block, cols), lambda d, t: (0, 0, chunk)),
                pl.BlockSpec((1, cols), lambda d, t: (0, chunk)),
            ],
            out_specs=[
                pl.BlockSpec((None, n_slots, block, cols), lambda d, t: (d, 0, 0, 0)),
                pl.BlockSpec((None, n_slots, block, HD), lambda d, t: (d, 0, 0, 0)),
            ],
        ),
        compiler_params=params(),
        cost_estimate=pl.CostEstimate(
            flops=12 * n_dp * n_slots * block * cols,
            bytes_accessed=2 * cols * block * (3 * blocks + n_dp * n_slots),
            transcendentals=0,
        ),
        name="join_partials",
    )(table, own, other, resid, head)


def place_kernel(count, order_ref, *refs):
    out_ref = refs[-1]
    for k in range(count):
        out_ref[:, order_ref[k]] = refs[k][...]


def place(order, pieces, whole, chunk, width):
    n_slots, block, cols = pieces[0].shape
    count = len(pieces)
    specs = [pl.BlockSpec((n_slots, block, cols), lambda i, o: (0, 0, 0)) for _ in pieces]
    operands = list(pieces)
    aliases = {}
    if whole is not None:
        specs.append(pl.BlockSpec(memory_space=pl.ANY))
        operands.append(whole)
        aliases = {1 + len(pieces): 0}
    return pl.pallas_call(
        functools.partial(place_kernel, count),
        out_shape=jax.ShapeDtypeStruct((n_slots, count, block, width), jnp.bfloat16),
        grid_spec=pltpu.PrefetchScalarGridSpec(
            num_scalar_prefetch=1,
            grid=(1,),
            in_specs=specs,
            out_specs=pl.BlockSpec((n_slots, count, block, cols), lambda i, o: (0, 0, 0, chunk)),
        ),
        input_output_aliases=aliases,
        compiler_params=params(),
        cost_estimate=pl.CostEstimate(
            flops=0, bytes_accessed=4 * n_slots * count * block * cols, transcendentals=0
        ),
        name="place_rows",
    )(order, *operands)


def on_device(responses, lengths, dest_dp, dest_slot, wq, wkv, wo, norm_gain, head_vec):
    n_sec = lax.axis_size("sec")
    n_dp = lax.axis_size("dp")
    n_tp = lax.axis_size("tp")
    _, local_len, width = responses.shape
    samples = lengths.shape[0]
    n_slots = 3 * samples // (2 * n_dp)
    seq = local_len * n_tp
    block = local_len // n_dp
    my_sec, my_dp, my_tp = lax.axis_index("sec"), lax.axis_index("dp"), lax.axis_index("tp")

    mine = responses[0]
    near = [mine] + [shift(mine, "tp", n_tp, k) for k in range(1, n_tp)]
    far_mine = swap(mine, "sec", n_sec, 2)
    half = local_len // 2
    far = [far_mine]
    for k in range(1, n_tp):
        upper = shift(far_mine[:half], "tp", n_tp, k)
        lower = swap(near[k][half:], "sec", n_sec, 2)
        far.append(jnp.concatenate([upper, lower], axis=0))
    near_pair = [swap(v, "sec", n_sec, 1) for v in near]
    far_pair = [swap(v, "sec", n_sec, 1) for v in far]
    batches = [near + near_pair, far + far_pair]

    quarter = lambda v, k: lax.dynamic_slice_in_dim(v, lax.rem(my_dp + k, n_dp) * block, block, 0)
    resid_0 = jnp.concatenate(
        [quarter(mine, 0)] + [shift(quarter(mine, k), "dp", n_dp, k) for k in range(1, n_dp)], axis=0
    )
    resid_0 = resid_0.reshape(n_dp, block, width)
    resid_2 = swap(resid_0, "sec", n_sec, 2)
    resid = jnp.concatenate(
        [resid_0, swap(resid_0, "sec", n_sec, 1), resid_2, swap(resid_2, "sec", n_sec, 1)], axis=0
    )

    owners = lax.rem(my_tp - jnp.arange(n_tp) + n_tp, n_tp)
    positions = (owners[:, None] * local_len + jnp.arange(local_len)[None, :]).reshape(seq)
    frequency = jnp.exp(jnp.arange(HD // 2, dtype=jnp.float32) * (-2.0 * math.log(ROPE_THETA) / HD))
    angles = positions.astype(jnp.float32)[:, None] * frequency[None, :]
    cos = jnp.tile(jnp.cos(angles), (1, 2))
    sin = jnp.concatenate([-jnp.sin(angles), jnp.sin(angles)], axis=1)
    mask = (positions[:, None] >= positions[None, :]).astype(jnp.float32)

    spread = []
    for rows in batches:
        ctx = attention(jnp.concatenate(rows, axis=0), norm_gain, cos, sin, mask, wq, wkv, n_dp, n_tp)
        for k in range(n_dp):
            piece = lax.dynamic_index_in_dim(ctx, lax.rem(my_dp + k, n_dp), 0, keepdims=False)
            spread.append(shift(piece, "dp", n_dp, k) if k else piece)
    q_width = wq.shape[2]
    ctx_rows = jnp.stack(spread, axis=1).reshape(-1, q_width)
    owned = ctx_rows.shape[0] // n_tp

    row_dp = lax.dynamic_index_in_dim(dest_dp, my_sec, 0, keepdims=False)
    row_slot = lax.dynamic_index_in_dim(dest_slot, my_sec, 0, keepdims=False)
    sample = jnp.arange(samples)
    i_rel = my_sec ^ (sample // n_dp)
    k_rel = lax.rem(my_dp - sample % n_dp + n_dp, n_dp)
    part_at = ((i_rel // 2) * n_dp + k_rel) * 2 + i_rel % 2
    resid_at = i_rel * n_dp + k_rel
    dests = lax.rem(my_dp + jnp.arange(n_dp), n_dp)
    chosen = (row_dp[None, None, :] == dests[:, None, None]) & (
        row_slot[None, None, :] == jnp.arange(n_slots)[None, :, None]
    )
    first_pos = my_tp * local_len + my_dp * block
    live = jnp.clip(lengths - first_pos, 0, block)
    pick = lambda v: jnp.sum(jnp.where(chosen, v[None, None, :], 0), axis=-1).reshape(-1)
    table = jnp.stack([pick(part_at), pick(resid_at), pick(live)]).astype(jnp.int32)
    order = lax.rem(my_dp - jnp.arange(n_dp) + n_dp, n_dp).astype(jnp.int32)

    cols = width // N_CHUNKS
    whole, stats = None, 0.0
    for chunk in range(N_CHUNKS):
        own, send = out_projection(ctx_rows, wo, owned, chunk, cols)
        own = own.reshape(-1, block, cols)
        send = send.reshape(n_tp - 1, -1, block, cols)
        other = jnp.stack([shift(send[k - 1], "tp", n_tp, n_tp - k) for k in range(1, n_tp)])
        packed, part_stats = join(table, own, other, resid, head_vec, chunk, n_dp, n_slots, block)
        stats = stats + part_stats[..., :2]
        pieces = [packed[0]] + [shift(packed[k], "dp", n_dp, k) for k in range(1, n_dp)]
        whole = place(order, pieces, whole, chunk, width)
    layer_out = jnp.transpose(whole.reshape(n_slots, local_len, width), (1, 0, 2))[None, None]

    token_scores = stats[..., 1] * lax.rsqrt(stats[..., 0] * (1.0 / width) + NORM_EPS)
    is_live = jnp.arange(block)[None, None, :] < table[2].reshape(n_dp, n_slots, 1)
    slot_sums = jnp.sum(jnp.where(is_live, token_scores, 0.0), axis=-1)
    by_sample = jnp.sum(jnp.where(chosen, slot_sums[:, :, None], 0.0), axis=(0, 1))
    by_model = jnp.where(jnp.arange(n_sec)[:, None] == my_sec, by_sample[None, :], 0.0)
    totals = lax.psum(by_model, ("sec", "dp", "tp"))
    averages = totals / lengths[None, :].astype(jnp.float32)
    owner = (dest_dp[n_sec - 1] == my_dp)[None, :] & (
        dest_slot[n_sec - 1][None, :] == jnp.arange(n_slots)[:, None]
    )
    sample_scores = jnp.sum(jnp.where(owner[:, None, :], averages[None, :, :], 0.0), axis=-1)
    return layer_out, sample_scores[None]


def solution(mesh):
    placed = (
        P(("sec", "dp"), "tp", None),
        P(),
        P(),
        P(),
        P("sec", None, "tp"),
        P("sec", None, None, "tp"),
        P("sec", "tp", None),
        P("sec", None),
        P("sec", None),
    )
    return jax.shard_map(
        on_device,
        mesh=mesh,
        in_specs=placed,
        out_specs=(P("sec", "dp", "tp", None, None), P("dp", None, None)),
        check_vma=False,
    )
```

```python
import functools
import math

import jax
import jax.numpy as jnp
from jax import lax
from jax.experimental import pallas as pl
from jax.experimental.pallas import tpu as pltpu
from jax.sharding import PartitionSpec as P

HD = 128
NORM_EPS = 1e-05
ROPE_THETA = 500000.0
VMEM_BYTES = 56 * 1024 * 1024
CHUNKS = (1, 1, 2, 2, 2)
AHEAD = 2


def params():
    return pltpu.CompilerParams(vmem_limit_bytes=VMEM_BYTES)


def swap(value, axis, size, step):
    return lax.ppermute(value, axis, [(j, j ^ step) for j in range(size)])


def shift(value, axis, size, step):
    return lax.ppermute(value, axis, [(j, (j + step) % size) for j in range(size)])


def attention_kernel(n_dp, n_tp, n_pieces, *refs):
    x_refs, refs = refs[:n_pieces], refs[n_pieces:]
    (gain_ref, cos_ref, sin_ref, mask_ref, wq_ref, wkv_ref, out_ref, normed, acc_q, acc_k, acc_v) = refs
    group, step = pl.program_id(0), pl.program_id(1)
    steps, rows, depth = normed.shape
    seq = mask_ref.shape[0]
    width = steps * depth

    @pl.when((group == 0) & (step == 0))
    def _():
        start = 0
        for x_ref in x_refs:
            size = min(16, x_ref.shape[0])

            def norm_rows(i, carry, x_ref=x_ref, start=start, size=size):
                x = x_ref[pl.ds(pl.multiple_of(i * size, size), size), :].astype(jnp.float32)
                inv = lax.rsqrt(jnp.sum(x * x, axis=-1, keepdims=True) * (1.0 / width) + NORM_EPS)
                y = (x * inv * gain_ref[...]).astype(jnp.bfloat16)
                to = pl.ds(pl.multiple_of(start + i * size, size), size)
                for j in range(steps):
                    normed[j, to, :] = y[:, j * depth : (j + 1) * depth]
                return carry

            lax.fori_loop(0, x_ref.shape[0] // size, norm_rows, 0)
            start += x_ref.shape[0]

    lhs = normed[step]
    part_q = jnp.dot(lhs, wq_ref[...], preferred_element_type=jnp.float32)
    part_k = jnp.dot(lhs, wkv_ref[0], preferred_element_type=jnp.float32)
    part_v = jnp.dot(lhs, wkv_ref[1], preferred_element_type=jnp.float32)

    @pl.when(step == 0)
    def _():
        acc_q[...] = part_q
        acc_k[...] = part_k
        acc_v[...] = part_v

    @pl.when(step > 0)
    def _():
        acc_q[...] += part_q
        acc_k[...] += part_k
        acc_v[...] += part_v

    @pl.when(step == steps - 1)
    def _():
        cos, sin = cos_ref[...], sin_ref[...]
        causal = jnp.concatenate([mask_ref[...]] * (acc_q.shape[1] // acc_k.shape[1]), axis=0) > 0.0
        block = seq // (n_dp * n_tp)
        kv_here = acc_k.shape[1] // HD
        per_kv = acc_q.shape[1] // acc_k.shape[1]

        def rope(v):
            return (v * cos + pltpu.roll(v, HD // 2, 1) * sin).astype(jnp.bfloat16)

        for s in range(rows // seq):
            at = slice(s * seq, (s + 1) * seq)
            for j in range(kv_here):
                cols = slice(j * HD, (j + 1) * HD)
                keys = rope(acc_k[at, cols])
                values = acc_v[at, cols].astype(jnp.bfloat16)
                heads = range(j * per_kv, (j + 1) * per_kv)
                queries = jnp.concatenate([rope(acc_q[at, h * HD : (h + 1) * HD]) for h in heads], axis=0)
                scores = lax.dot_general(
                    queries, keys, (((1,), (1,)), ((), ())), preferred_element_type=jnp.float32
                ) * (1.0 / math.sqrt(HD))
                scores = jnp.where(causal, scores, -1e30)
                expo = jnp.exp(scores - jnp.max(scores, axis=-1, keepdims=True))
                weights = (expo / jnp.sum(expo, axis=-1, keepdims=True)).astype(jnp.bfloat16)
                context = jnp.dot(weights, values, preferred_element_type=jnp.float32).astype(jnp.bfloat16)
                for n, h in enumerate(heads):
                    for t in range(n_tp):
                        for z in range(n_dp):
                            start = n * seq + (t * n_dp + z) * block
                            out_ref[z, t, s, :, h * HD : (h + 1) * HD] = context[start : start + block]


def attention(pieces, gain, cos, sin, mask, wq, wkv, n_dp, n_tp):
    rows, width = sum(p.shape[0] for p in pieces), pieces[0].shape[1]
    seq = mask.shape[0]
    q_width, kv_width = wq.shape[2], wkv.shape[3]
    kv_block = min(2 * HD, kv_width)
    groups = kv_width // kv_block
    q_block = q_width // groups
    steps = 2
    depth = width // steps
    samples = rows // seq
    block = seq // (n_dp * n_tp)
    fixed = lambda g, k: (0, 0)
    return pl.pallas_call(
        functools.partial(attention_kernel, n_dp, n_tp, len(pieces)),
        out_shape=jax.ShapeDtypeStruct((n_dp, n_tp, samples, block, q_width), jnp.bfloat16),
        grid=(groups, steps),
        in_specs=[pl.BlockSpec(p.shape, fixed) for p in pieces]
        + [
            pl.BlockSpec((1, width), fixed),
            pl.BlockSpec((seq, HD), fixed),
            pl.BlockSpec((seq, HD), fixed),
            pl.BlockSpec((seq, seq), fixed),
            pl.BlockSpec((None, depth, q_block), lambda g, k: (0, k, g)),
            pl.BlockSpec((None, 2, depth, kv_block), lambda g, k: (0, 0, k, g)),
        ],
        out_specs=pl.BlockSpec((n_dp, n_tp, samples, block, q_block), lambda g, k: (0, 0, 0, 0, g)),
        scratch_shapes=[
            pltpu.VMEM((steps, rows, depth), jnp.bfloat16),
            pltpu.VMEM((rows, q_block), jnp.float32),
            pltpu.VMEM((rows, kv_block), jnp.float32),
            pltpu.VMEM((rows, kv_block), jnp.float32),
        ],
        compiler_params=params(),
        cost_estimate=pl.CostEstimate(flops=1, bytes_accessed=1, transcendentals=0),
        name="project_and_attend",
    )(*pieces, gain, cos, sin, mask, wq, wkv)


def out_kernel(ctx_ref, wo_ref, own_ref, send_ref):
    full = jnp.dot(ctx_ref[...], wo_ref[...], preferred_element_type=jnp.float32).astype(jnp.bfloat16)
    mine = own_ref.shape[0]
    own_ref[...] = full[:mine]
    send_ref[...] = full[mine:]


def out_projection(ctx, wo, mine, first, cols):
    rows, depth = ctx.shape
    col_block = min(512, cols)
    inner = cols // col_block
    base = first // col_block
    return pl.pallas_call(
        out_kernel,
        out_shape=[
            jax.ShapeDtypeStruct((mine, cols), jnp.bfloat16),
            jax.ShapeDtypeStruct((rows - mine, cols), jnp.bfloat16),
        ],
        grid=(inner,),
        in_specs=[
            pl.BlockSpec((rows, depth), lambda n: (0, 0)),
            pl.BlockSpec((None, depth, col_block), lambda n: (0, 0, base + n)),
        ],
        out_specs=[
            pl.BlockSpec((mine, col_block), lambda n: (0, n)),
            pl.BlockSpec((rows - mine, col_block), lambda n: (0, n)),
        ],
        compiler_params=params(),
        cost_estimate=pl.CostEstimate(flops=1, bytes_accessed=1, transcendentals=0),
        name="out_projection",
    )(ctx, wo)


def join_kernel(n_slots, block, table_ref, own_ref, other_ref, resid_ref, head_ref, packed_ref, stats_ref):
    dest = pl.program_id(0)
    head = head_ref[...]
    lane = lax.broadcasted_iota(jnp.int32, (block, HD), 1)
    row = lax.broadcasted_iota(jnp.int32, (block, 1), 0)

    for slot in range(n_slots):
        entry = dest * n_slots + slot
        part, resid, live = table_ref[0, entry], table_ref[1, entry], table_ref[2, entry]
        added = own_ref[part].astype(jnp.float32)
        for k in range(other_ref.shape[0]):
            added = added + other_ref[k, part].astype(jnp.float32)
        hidden = resid_ref[resid].astype(jnp.float32) + added
        packed_ref[slot] = jnp.where(row < live, hidden, 0.0).astype(jnp.bfloat16)
        squares = jnp.sum(hidden * hidden, axis=-1, keepdims=True)
        scored = jnp.sum(hidden * head, axis=-1, keepdims=True)
        stats_ref[slot] = jnp.where(lane == 0, squares, jnp.where(lane == 1, scored, 0.0))


def join(table, own, other, resid, head, chunk, n_dp, n_slots, block):
    blocks, _, cols = own.shape
    return pl.pallas_call(
        functools.partial(join_kernel, n_slots, block),
        out_shape=[
            jax.ShapeDtypeStruct((n_dp, n_slots, block, cols), jnp.bfloat16),
            jax.ShapeDtypeStruct((n_dp, n_slots, block, HD), jnp.float32),
        ],
        grid_spec=pltpu.PrefetchScalarGridSpec(
            num_scalar_prefetch=1,
            grid=(n_dp,),
            in_specs=[
                pl.BlockSpec(own.shape, lambda d, t: (0, 0, 0)),
                pl.BlockSpec(other.shape, lambda d, t: (0, 0, 0, 0)),
                pl.BlockSpec((blocks, block, cols), lambda d, t: (0, 0, chunk)),
                pl.BlockSpec((1, cols), lambda d, t: (0, chunk)),
            ],
            out_specs=[
                pl.BlockSpec((None, n_slots, block, cols), lambda d, t: (d, 0, 0, 0)),
                pl.BlockSpec((None, n_slots, block, HD), lambda d, t: (d, 0, 0, 0)),
            ],
        ),
        compiler_params=params(),
        cost_estimate=pl.CostEstimate(flops=1, bytes_accessed=1, transcendentals=0),
        name="join_partials",
    )(table, own, other, resid, head)


def place_kernel(sizes, count, order_ref, *refs):
    out_ref = refs[-1]
    step = pl.program_id(1)
    first = 0
    for chunk, size in enumerate(sizes):
        @pl.when((step >= first) & (step < first + size))
        def _(chunk=chunk):
            for k in range(count):
                out_ref[:, order_ref[k]] = refs[chunk * count + k][...]

        first += size


def place(order, arrived, sizes, width):
    n_slots, block, _ = arrived[0][0].shape
    count = len(arrived[0])
    unit = width // sum(sizes)
    rows = n_slots // 2
    firsts = [sum(sizes[:c]) for c in range(len(sizes))]

    def spec(first, size):
        return pl.BlockSpec((rows, block, unit), lambda h, c, o: (h, 0, jnp.clip(c - first, 0, size - 1)))

    return pl.pallas_call(
        functools.partial(place_kernel, sizes, count),
        out_shape=jax.ShapeDtypeStruct((n_slots, count, block, width), jnp.bfloat16),
        grid_spec=pltpu.PrefetchScalarGridSpec(
            num_scalar_prefetch=1,
            grid=(n_slots // rows, sum(sizes)),
            in_specs=[spec(f, s) for f, s in zip(firsts, sizes) for _ in range(count)],
            out_specs=pl.BlockSpec((rows, count, block, unit), lambda h, c, o: (h, 0, 0, c)),
        ),
        compiler_params=params(),
        cost_estimate=pl.CostEstimate(flops=1, bytes_accessed=1, transcendentals=0),
        name="place_rows",
    )(order, *[piece for pieces in arrived for piece in pieces])


def on_device(responses, lengths, dest_dp, dest_slot, wq, wkv, wo, norm_gain, head_vec):
    n_sec = lax.axis_size("sec")
    n_dp = lax.axis_size("dp")
    n_tp = lax.axis_size("tp")
    _, local_len, width = responses.shape
    samples = lengths.shape[0]
    n_slots = 3 * samples // (2 * n_dp)
    seq = local_len * n_tp
    block = local_len // n_dp
    my_sec, my_dp, my_tp = lax.axis_index("sec"), lax.axis_index("dp"), lax.axis_index("tp")

    mine = responses[0]
    near = [mine] + [shift(mine, "tp", n_tp, k) for k in range(1, n_tp)]
    far_mine = swap(mine, "sec", n_sec, 2)
    half = local_len // 2
    far = [far_mine]
    for k in range(1, n_tp):
        parts = [shift(far_mine[:half], "tp", n_tp, k), swap(near[k][half:], "sec", n_sec, 2)]
        far += parts if half % 16 == 0 else [jnp.concatenate(parts, axis=0)]
    near = near + [swap(v, "sec", n_sec, 1) for v in near]
    far = far + [swap(v, "sec", n_sec, 1) for v in far]

    def quarters(v):
        part = lambda k: lax.dynamic_slice_in_dim(v, lax.rem(my_dp + k, n_dp) * block, block, 0)
        return jnp.stack([part(0)] + [shift(part(k), "dp", n_dp, k) for k in range(1, n_dp)])

    resid_0, resid_2 = quarters(mine), quarters(far_mine)

    owners = lax.rem(my_tp - jnp.arange(n_tp) + n_tp, n_tp)
    positions = (owners[:, None] * local_len + jnp.arange(local_len)[None, :]).reshape(seq)
    frequency = jnp.exp(jnp.arange(HD // 2, dtype=jnp.float32) * (-2.0 * math.log(ROPE_THETA) / HD))
    angles = positions.astype(jnp.float32)[:, None] * frequency[None, :]
    cos = jnp.tile(jnp.cos(angles), (1, 2))
    sin = jnp.concatenate([-jnp.sin(angles), jnp.sin(angles)], axis=1)
    mask = (positions[:, None] >= positions[None, :]).astype(jnp.float32)

    def spread(pieces):
        ctx = attention(pieces, norm_gain, cos, sin, mask, wq, wkv, n_dp, n_tp)
        here = lambda k: lax.dynamic_index_in_dim(ctx, lax.rem(my_dp + k, n_dp), 0, keepdims=False)
        parts = [here(0)] + [shift(here(k), "dp", n_dp, k) for k in range(1, n_dp)]
        return ctx, parts

    first_ctx, first_parts = spread(near)
    resid = jnp.concatenate(
        [resid_0, swap(resid_0, "sec", n_sec, 1), resid_2, swap(resid_2, "sec", n_sec, 1)], axis=0
    )
    far, first_ctx, resid = lax.optimization_barrier((far, first_ctx, resid))
    _, second_parts = spread(far)
    q_width = wq.shape[2]
    ctx_rows = jnp.stack(first_parts + second_parts, axis=1).reshape(-1, q_width)
    owned = ctx_rows.shape[0] // n_tp

    row_dp = lax.dynamic_index_in_dim(dest_dp, my_sec, 0, keepdims=False)
    row_slot = lax.dynamic_index_in_dim(dest_slot, my_sec, 0, keepdims=False)
    sample = jnp.arange(samples)
    i_rel = my_sec ^ (sample // n_dp)
    k_rel = lax.rem(my_dp - sample % n_dp + n_dp, n_dp)
    part_at = ((i_rel // 2) * n_dp + k_rel) * 2 + i_rel % 2
    resid_at = i_rel * n_dp + k_rel
    dests = lax.rem(my_dp + jnp.arange(n_dp), n_dp)
    chosen = (row_dp[None, None, :] == dests[:, None, None]) & (
        row_slot[None, None, :] == jnp.arange(n_slots)[None, :, None]
    )
    first_pos = my_tp * local_len + my_dp * block
    live = jnp.clip(lengths - first_pos, 0, block)
    pick = lambda v: jnp.sum(jnp.where(chosen, v[None, None, :], 0), axis=-1).reshape(-1)
    table = jnp.stack([pick(part_at), pick(resid_at), pick(live)]).astype(jnp.int32)
    order = lax.rem(my_dp - jnp.arange(n_dp) + n_dp, n_dp).astype(jnp.int32)

    unit = width // sum(CHUNKS)
    starts = [unit * sum(CHUNKS[:c]) for c in range(len(CHUNKS))]
    stats, arrived, owns, sends = [], [], [], []

    def project(ctx_from):
        own, send = out_projection(ctx_from, wo, owned, starts[len(owns)], unit * CHUNKS[len(owns)])
        owns.append(own.reshape(-1, block, own.shape[-1]))
        sends.append(send.reshape(n_tp - 1, -1, block, own.shape[-1]))

    for _ in range(AHEAD):
        project(ctx_rows)
        ctx_rows, owns[-1] = lax.optimization_barrier((ctx_rows, owns[-1]))
    for chunk, size in enumerate(CHUNKS):
        other = [shift(sends[chunk][k - 1], "tp", n_tp, n_tp - k) for k in range(1, n_tp)]
        own = owns[chunk]
        last = min(chunk + AHEAD, len(CHUNKS)) - 1
        if last > chunk:
            own, sends[last] = lax.optimization_barrier((own, sends[last]))
        if chunk >= 2:
            own, arrived[chunk - 2] = lax.optimization_barrier((own, arrived[chunk - 2]))
        packed, part_stats = join(
            table, own, jnp.stack(other), resid, head_vec, starts[chunk] // (unit * size), n_dp, n_slots, block
        )
        if chunk + AHEAD < len(CHUNKS):
            packed, ctx_rows = lax.optimization_barrier((packed, ctx_rows))
            project(ctx_rows)
        stats.append(part_stats)
        arrived.append([packed[0]] + [shift(packed[k], "dp", n_dp, k) for k in range(1, n_dp)])
    arrived[-2], stats[-1] = lax.optimization_barrier((arrived[-2], stats[-1]))
    whole = place(order, arrived, CHUNKS, width)
    layer_out = jnp.transpose(whole.reshape(n_slots, local_len, width), (1, 0, 2))[None, None]

    stats = sum(v[..., :2] for v in stats)
    token_scores = stats[..., 1] * lax.rsqrt(stats[..., 0] * (1.0 / width) + NORM_EPS)
    is_live = jnp.arange(block)[None, None, :] < table[2].reshape(n_dp, n_slots, 1)
    slot_sums = jnp.sum(jnp.where(is_live, token_scores, 0.0), axis=-1)
    by_sample = jnp.sum(jnp.where(chosen, slot_sums[:, :, None], 0.0), axis=(0, 1))
    by_model = jnp.where(jnp.arange(n_sec)[:, None] == my_sec, by_sample[None, :], 0.0)
    for axis, size in (("tp", n_tp), ("dp", n_dp), ("sec", n_sec)):
        by_model = sum([shift(by_model, axis, size, k) for k in range(1, size)], by_model)
    totals = by_model
    averages = totals / lengths[None, :].astype(jnp.float32)
    owner = (dest_dp[n_sec - 1] == my_dp)[None, :] & (
        dest_slot[n_sec - 1][None, :] == jnp.arange(n_slots)[:, None]
    )
    sample_scores = jnp.sum(jnp.where(owner[:, None, :], averages[None, :, :], 0.0), axis=-1)
    return layer_out, sample_scores[None]


def solution(mesh):
    placed = (
        P(("sec", "dp"), "tp", None),
        P(),
        P(),
        P(),
        P("sec", None, "tp"),
        P("sec", None, None, "tp"),
        P("sec", "tp", None),
        P("sec", None),
        P("sec", None),
    )
    return jax.shard_map(
        on_device,
        mesh=mesh,
        in_specs=placed,
        out_specs=(P("sec", "dp", "tp", None, None), P("dp", None, None)),
        check_vma=False,
    )
```

```python
import functools
import math

import jax
import jax.numpy as jnp
from jax import lax
from jax.experimental import pallas as pl
from jax.experimental.pallas import tpu as pltpu
from jax.sharding import PartitionSpec as P

HD = 128
NORM_EPS = 1e-05
ROPE_THETA = 500000.0
VMEM_BYTES = 56 * 1024 * 1024
CHUNKS = (1, 1, 2, 2, 2)


def params():
    return pltpu.CompilerParams(vmem_limit_bytes=VMEM_BYTES)


def swap(value, axis, size, step):
    return lax.ppermute(value, axis, [(j, j ^ step) for j in range(size)])


sync = lax.optimization_barrier


def shift(value, axis, size, step):
    return lax.ppermute(value, axis, [(j, (j + step) % size) for j in range(size)])


def attention_kernel(n_dp, n_tp, n_pieces, *refs):
    x_refs, refs = refs[:n_pieces], refs[n_pieces:]
    (gain_ref, cos_ref, sin_ref, mask_ref, wq_ref, wkv_ref, out_ref, normed, acc_q, acc_k, acc_v) = refs
    group, step = pl.program_id(0), pl.program_id(1)
    steps, rows, depth = normed.shape
    seq = mask_ref.shape[0]
    width = steps * depth

    @pl.when((group == 0) & (step == 0))
    def _():
        start = 0
        for x_ref in x_refs:
            size = min(16, x_ref.shape[0])

            def norm_rows(i, carry, x_ref=x_ref, start=start, size=size):
                x = x_ref[pl.ds(pl.multiple_of(i * size, size), size), :].astype(jnp.float32)
                inv = lax.rsqrt(jnp.sum(x * x, axis=-1, keepdims=True) * (1.0 / width) + NORM_EPS)
                y = (x * inv * gain_ref[...]).astype(jnp.bfloat16)
                to = pl.ds(pl.multiple_of(start + i * size, size), size)
                for j in range(steps):
                    normed[j, to, :] = y[:, j * depth : (j + 1) * depth]
                return carry

            lax.fori_loop(0, x_ref.shape[0] // size, norm_rows, 0)
            start += x_ref.shape[0]

    lhs = normed[step]
    part_q = jnp.dot(lhs, wq_ref[...], preferred_element_type=jnp.float32)
    part_k = jnp.dot(lhs, wkv_ref[0], preferred_element_type=jnp.float32)
    part_v = jnp.dot(lhs, wkv_ref[1], preferred_element_type=jnp.float32)

    @pl.when(step == 0)
    def _():
        acc_q[...] = part_q
        acc_k[...] = part_k
        acc_v[...] = part_v

    @pl.when(step > 0)
    def _():
        acc_q[...] += part_q
        acc_k[...] += part_k
        acc_v[...] += part_v

    @pl.when(step == steps - 1)
    def _():
        cos, sin = cos_ref[...], sin_ref[...]
        causal = jnp.concatenate([mask_ref[...]] * (acc_q.shape[1] // acc_k.shape[1]), axis=0) > 0.0
        block = seq // (n_dp * n_tp)
        kv_here = acc_k.shape[1] // HD
        per_kv = acc_q.shape[1] // acc_k.shape[1]

        def rope(v):
            return (v * cos + pltpu.roll(v, HD // 2, 1) * sin).astype(jnp.bfloat16)

        for s in range(rows // seq):
            at = slice(s * seq, (s + 1) * seq)
            for j in range(kv_here):
                cols = slice(j * HD, (j + 1) * HD)
                keys = rope(acc_k[at, cols])
                values = acc_v[at, cols].astype(jnp.bfloat16)
                heads = range(j * per_kv, (j + 1) * per_kv)
                queries = jnp.concatenate([rope(acc_q[at, h * HD : (h + 1) * HD]) for h in heads], axis=0)
                scores = lax.dot_general(
                    queries, keys, (((1,), (1,)), ((), ())), preferred_element_type=jnp.float32
                ) * (1.0 / math.sqrt(HD))
                scores = jnp.where(causal, scores, -1e30)
                expo = jnp.exp(scores - jnp.max(scores, axis=-1, keepdims=True))
                weights = (expo / jnp.sum(expo, axis=-1, keepdims=True)).astype(jnp.bfloat16)
                context = jnp.dot(weights, values, preferred_element_type=jnp.float32).astype(jnp.bfloat16)
                for n, h in enumerate(heads):
                    for t in range(n_tp):
                        for z in range(n_dp):
                            start = n * seq + (t * n_dp + z) * block
                            out_ref[z, t, s, :, h * HD : (h + 1) * HD] = context[start : start + block]


def attention(pieces, gain, cos, sin, mask, wq, wkv, n_dp, n_tp):
    rows, width = sum(p.shape[0] for p in pieces), pieces[0].shape[1]
    seq = mask.shape[0]
    q_width, kv_width = wq.shape[2], wkv.shape[3]
    kv_block = min(2 * HD, kv_width)
    groups = kv_width // kv_block
    q_block = q_width // groups
    steps = 2
    depth = width // steps
    samples = rows // seq
    block = seq // (n_dp * n_tp)
    fixed = lambda g, k: (0, 0)
    return pl.pallas_call(
        functools.partial(attention_kernel, n_dp, n_tp, len(pieces)),
        out_shape=jax.ShapeDtypeStruct((n_dp, n_tp, samples, block, q_width), jnp.bfloat16),
        grid=(groups, steps),
        in_specs=[pl.BlockSpec(p.shape, fixed) for p in pieces]
        + [
            pl.BlockSpec((1, width), fixed),
            pl.BlockSpec((seq, HD), fixed),
            pl.BlockSpec((seq, HD), fixed),
            pl.BlockSpec((seq, seq), fixed),
            pl.BlockSpec((None, depth, q_block), lambda g, k: (0, k, g)),
            pl.BlockSpec((None, 2, depth, kv_block), lambda g, k: (0, 0, k, g)),
        ],
        out_specs=pl.BlockSpec((n_dp, n_tp, samples, block, q_block), lambda g, k: (0, 0, 0, 0, g)),
        scratch_shapes=[
            pltpu.VMEM((steps, rows, depth), jnp.bfloat16),
            pltpu.VMEM((rows, q_block), jnp.float32),
            pltpu.VMEM((rows, kv_block), jnp.float32),
            pltpu.VMEM((rows, kv_block), jnp.float32),
        ],
        compiler_params=params(),
        cost_estimate=pl.CostEstimate(flops=1, bytes_accessed=1, transcendentals=0),
        name="project_and_attend",
    )(*pieces, gain, cos, sin, mask, wq, wkv)


def out_kernel(ctx_ref, wo_ref, own_ref, send_ref):
    full = jnp.dot(ctx_ref[...], wo_ref[...], preferred_element_type=jnp.float32).astype(jnp.bfloat16)
    mine = own_ref.shape[0]
    own_ref[...] = full[:mine]
    send_ref[...] = full[mine:]


def out_projection(ctx, wo, mine, first, cols):
    rows, depth = ctx.shape
    col_block = min(512, cols)
    inner = cols // col_block
    base = first // col_block
    return pl.pallas_call(
        out_kernel,
        out_shape=[
            jax.ShapeDtypeStruct((mine, cols), jnp.bfloat16),
            jax.ShapeDtypeStruct((rows - mine, cols), jnp.bfloat16),
        ],
        grid=(inner,),
        in_specs=[
            pl.BlockSpec((rows, depth), lambda n: (0, 0)),
            pl.BlockSpec((None, depth, col_block), lambda n: (0, 0, base + n)),
        ],
        out_specs=[
            pl.BlockSpec((mine, col_block), lambda n: (0, n)),
            pl.BlockSpec((rows - mine, col_block), lambda n: (0, n)),
        ],
        compiler_params=params(),
        cost_estimate=pl.CostEstimate(flops=1, bytes_accessed=1, transcendentals=0),
        name="out_projection",
    )(ctx, wo)


def join_kernel(n_slots, block, table_ref, near_ref, far_ref, near_other, far_other, resid_ref, pair_ref, head_ref, *out_refs):
    packed_refs, stats_ref = out_refs[:-1], out_refs[-1]
    head = head_ref[...]
    lane = lax.broadcasted_iota(jnp.int32, (block, HD), 1)
    row = lax.broadcasted_iota(jnp.int32, (block, 1), 0)
    step = pl.program_id(0)
    slots = packed_refs[0].shape[0]

    for dest, packed_ref in enumerate(packed_refs):
        for slot in range(slots):
            entry = dest * n_slots + step * slots + slot
            part, resid, live = table_ref[0, entry], table_ref[1, entry], table_ref[2, entry]
            is_far = table_ref[4, entry] > 0
            added = jnp.where(is_far, far_ref[part], near_ref[part]).astype(jnp.float32)
            for k in range(near_other.shape[0]):
                added = added + jnp.where(is_far, far_other[k, part], near_other[k, part]).astype(jnp.float32)
            rows_in = jnp.where(table_ref[3, entry] > 0, pair_ref[resid], resid_ref[resid])
            hidden = rows_in.astype(jnp.float32) + added
            packed_ref[slot] = jnp.where(row < live, hidden, 0.0).astype(jnp.bfloat16)
            squares = jnp.sum(hidden * hidden, axis=-1, keepdims=True)
            scored = jnp.sum(hidden * head, axis=-1, keepdims=True)
            stats_ref[dest, slot] = jnp.where(lane == 0, squares, jnp.where(lane == 1, scored, 0.0))


def join(table, owns, others, resid, resid_pair, head, chunk, n_dp, n_slots, block):
    cols = owns[0].shape[-1]
    slots = n_slots // 2
    fixed = lambda i, t: (0, 0, 0)
    here = lambda i, t: (0, 0, chunk)
    out = pl.pallas_call(
        functools.partial(join_kernel, n_slots, block),
        out_shape=[jax.ShapeDtypeStruct((n_slots, block, cols), jnp.bfloat16) for _ in range(n_dp)]
        + [jax.ShapeDtypeStruct((n_dp, n_slots, block, HD), jnp.float32)],
        grid_spec=pltpu.PrefetchScalarGridSpec(
            num_scalar_prefetch=1,
            grid=(n_slots // slots,),
            in_specs=[
                pl.BlockSpec(owns[0].shape, fixed),
                pl.BlockSpec(owns[1].shape, fixed),
                pl.BlockSpec(others[0].shape, lambda i, t: (0, 0, 0, 0)),
                pl.BlockSpec(others[1].shape, lambda i, t: (0, 0, 0, 0)),
                pl.BlockSpec((resid.shape[0], block, cols), here),
                pl.BlockSpec((resid.shape[0], block, cols), here),
                pl.BlockSpec((1, cols), lambda i, t: (0, chunk)),
            ],
            out_specs=[pl.BlockSpec((slots, block, cols), lambda i, t: (i, 0, 0)) for _ in range(n_dp)]
            + [pl.BlockSpec((n_dp, slots, block, HD), lambda i, t: (0, i, 0, 0))],
        ),
        compiler_params=params(),
        cost_estimate=pl.CostEstimate(flops=1, bytes_accessed=1, transcendentals=0),
        name="join_partials",
    )(table, *owns, *others, resid, resid_pair, head)
    return list(out[:-1]), out[-1]


def place_kernel(count, order_ref, *refs):
    out_ref = refs[-1]
    for k in range(count):
        out_ref[:, order_ref[k]] = refs[k][...]


def place(order, pieces, whole, chunk, width):
    n_slots, block, cols = pieces[0].shape
    count = len(pieces)
    rows = n_slots // 3
    specs = [pl.BlockSpec((rows, block, cols), lambda i, o: (i, 0, 0)) for _ in pieces]
    operands = list(pieces)
    aliases = {}
    if whole is not None:
        specs.append(pl.BlockSpec(memory_space=pl.ANY))
        operands.append(whole)
        aliases = {1 + count: 0}
    return pl.pallas_call(
        functools.partial(place_kernel, count),
        out_shape=jax.ShapeDtypeStruct((n_slots, count, block, width), jnp.bfloat16),
        grid_spec=pltpu.PrefetchScalarGridSpec(
            num_scalar_prefetch=1,
            grid=(n_slots // rows,),
            in_specs=specs,
            out_specs=pl.BlockSpec((rows, count, block, cols), lambda i, o: (i, 0, 0, chunk)),
        ),
        input_output_aliases=aliases,
        compiler_params=params(),
        cost_estimate=pl.CostEstimate(flops=1, bytes_accessed=1, transcendentals=0),
        name="place_rows",
    )(order, *operands)


def on_device(responses, lengths, dest_dp, dest_slot, wq, wkv, wo, norm_gain, head_vec):
    n_sec = lax.axis_size("sec")
    n_dp = lax.axis_size("dp")
    n_tp = lax.axis_size("tp")
    _, local_len, width = responses.shape
    samples = lengths.shape[0]
    n_slots = 3 * samples // (2 * n_dp)
    seq = local_len * n_tp
    block = local_len // n_dp
    my_sec, my_dp, my_tp = lax.axis_index("sec"), lax.axis_index("dp"), lax.axis_index("tp")

    owners = lax.rem(my_tp - jnp.arange(n_tp) + n_tp, n_tp)
    positions = (owners[:, None] * local_len + jnp.arange(local_len)[None, :]).reshape(seq)
    frequency = jnp.exp(jnp.arange(HD // 2, dtype=jnp.float32) * (-2.0 * math.log(ROPE_THETA) / HD))
    angles = positions.astype(jnp.float32)[:, None] * frequency[None, :]
    cos = jnp.tile(jnp.cos(angles), (1, 2))
    sin = jnp.concatenate([-jnp.sin(angles), jnp.sin(angles)], axis=1)
    mask = (positions[:, None] >= positions[None, :]).astype(jnp.float32)

    mine = responses[0]
    quarter = lambda k: lax.dynamic_slice_in_dim(mine, lax.rem(my_dp + k, n_dp) * block, block, 0)
    resid = [quarter(0)] + [shift(quarter(k), "dp", n_dp, k) for k in range(1, n_dp)]
    near = [mine] + [shift(mine, "tp", n_tp, k) for k in range(1, n_tp)]
    far_mine = swap(mine, "sec", n_sec, 2)
    near, far_mine, resid, cos, sin, mask = sync((near, far_mine, resid, cos, sin, mask))

    half = local_len // 2
    far = [far_mine]
    for k in range(1, n_tp):
        parts = [shift(far_mine[:half], "tp", n_tp, k), swap(near[k][half:], "sec", n_sec, 2)]
        far += parts if half % 16 == 0 else [jnp.concatenate(parts, axis=0)]
    near_pair = [swap(v, "sec", n_sec, 1) for v in near]
    resid = jnp.stack(resid)
    far, near, near_pair, resid = sync((far, near, near_pair, resid))

    attend = lambda pieces: attention(pieces, norm_gain, cos, sin, mask, wq, wkv, n_dp, n_tp)

    def spread(ctx):
        here = lambda k: lax.dynamic_index_in_dim(ctx, lax.rem(my_dp + k, n_dp), 0, keepdims=False)
        return [here(0)] + [shift(here(k), "dp", n_dp, k) for k in range(1, n_dp)]

    def gathered(parts):
        return jnp.stack(parts, axis=1).reshape(-1, wq.shape[2])

    near_ctx = attend(near + near_pair)
    far_pair = [swap(v, "sec", n_sec, 1) for v in far]
    resid_far = swap(resid, "sec", n_sec, 2)
    near_ctx, far, far_pair, resid, resid_far = sync((near_ctx, far, far_pair, resid, resid_far))
    near_rows = spread(near_ctx)
    resid = jnp.concatenate([resid, resid_far], axis=0)
    resid_pair = swap(resid, "sec", n_sec, 1)
    far_ctx = attend(far + far_pair)
    near_rows, far_ctx, resid, resid_pair = sync((near_rows, far_ctx, resid, resid_pair))

    row_dp = lax.dynamic_index_in_dim(dest_dp, my_sec, 0, keepdims=False)
    row_slot = lax.dynamic_index_in_dim(dest_slot, my_sec, 0, keepdims=False)
    sample = jnp.arange(samples)
    i_rel = my_sec ^ (sample // n_dp)
    k_rel = lax.rem(my_dp - sample % n_dp + n_dp, n_dp)
    part_at = k_rel * 2 + i_rel % 2
    resid_at = (i_rel // 2) * n_dp + k_rel
    dests = lax.rem(my_dp + jnp.arange(n_dp), n_dp)
    chosen = (row_dp[None, None, :] == dests[:, None, None]) & (
        row_slot[None, None, :] == jnp.arange(n_slots)[None, :, None]
    )
    first_pos = my_tp * local_len + my_dp * block
    live = jnp.clip(lengths - first_pos, 0, block)
    pick = lambda v: jnp.sum(jnp.where(chosen, v[None, None, :], 0), axis=-1).reshape(-1)
    table = jnp.stack([pick(part_at), pick(resid_at), pick(live), pick(i_rel % 2), pick(i_rel // 2)]).astype(jnp.int32)
    order = lax.rem(my_dp - jnp.arange(n_dp) + n_dp, n_dp).astype(jnp.int32)

    unit = width // sum(CHUNKS)
    starts = [unit * sum(CHUNKS[:c]) for c in range(len(CHUNKS))]
    count = len(CHUNKS)

    def project(chunk, ctx_rows):
        owned = ctx_rows.shape[0] // n_tp
        own, send = out_projection(ctx_rows, wo, owned, starts[chunk], unit * CHUNKS[chunk])
        own = own.reshape(-1, block, own.shape[-1])
        return own, send.reshape(n_tp - 1, -1, block, own.shape[-1])

    def exchange(projected):
        send = projected[1]
        return jnp.stack([shift(send[k - 1], "tp", n_tp, n_tp - k) for k in range(1, n_tp)])

    def finish(chunk, owns, others):
        return join(
            table, owns, others, resid, resid_pair, head_vec, starts[chunk] // (unit * CHUNKS[chunk]),
            n_dp, n_slots, block,
        )

    def put(whole, chunk, pieces):
        return place(order, pieces, whole, starts[chunk] // (unit * CHUNKS[chunk]), width)

    far_rows = spread(far_ctx)
    near_rows = gathered(near_rows)
    first = [project(c, near_rows) for c in range(2)]
    first, near_rows = sync((first, near_rows))
    near_others = [exchange(p) for p in first]
    near_projected = first + [project(c, near_rows) for c in range(2, count)]
    far_rows, near_others, near_projected = sync((far_rows, near_others, near_projected))

    far_rows = gathered(far_rows)
    first = project(0, far_rows)
    first, far_rows = sync((first, far_rows))
    far_others = [exchange(first)]
    far_projected = [first, project(1, far_rows)]
    far_others, far_projected, far_rows = sync((far_others, far_projected, far_rows))
    packed, part = finish(0, [near_projected[0][0], first[0]], [near_others[0], far_others[0]])
    packed, far_projected, far_rows = sync((packed, far_projected, far_rows))

    stats, whole, pieces = [part], None, None
    for chunk in range(count):
        moved = [packed[0]] + [shift(packed[k], "dp", n_dp, k) for k in range(1, n_dp)]
        if pieces is not None:
            whole = put(whole, chunk - 1, pieces)
        ahead = chunk + 1
        if ahead < count:
            far_others.append(exchange(far_projected[ahead]))
            if ahead + 1 < count:
                near_others.append(exchange(near_projected[ahead + 1]))
                far_projected.append(project(ahead + 1, far_rows))
            owns = [near_projected[ahead][0], far_projected[ahead][0]]
            packed, part = finish(ahead, owns, [near_others[ahead], far_others[ahead]])
            stats.append(part)
            moved, packed, whole, far_rows, far_projected, near_others[-1] = sync(
                (moved, packed, whole, far_rows, far_projected, near_others[-1])
            )
        pieces = moved
    whole = put(whole, count - 1, pieces)
    layer_out = jnp.transpose(whole.reshape(n_slots, local_len, width), (1, 0, 2))[None, None]

    stats = sum(v[..., :2] for v in stats)
    token_scores = stats[..., 1] * lax.rsqrt(stats[..., 0] * (1.0 / width) + NORM_EPS)
    is_live = jnp.arange(block)[None, None, :] < table[2].reshape(n_dp, n_slots, 1)
    slot_sums = jnp.sum(jnp.where(is_live, token_scores, 0.0), axis=-1)
    by_sample = jnp.sum(jnp.where(chosen, slot_sums[:, :, None], 0.0), axis=(0, 1))
    by_model = jnp.where(jnp.arange(n_sec)[:, None] == my_sec, by_sample[None, :], 0.0)
    for axis, size in (("tp", n_tp), ("dp", n_dp), ("sec", n_sec)):
        by_model = sum([shift(by_model, axis, size, k) for k in range(1, size)], by_model)
    totals = by_model
    averages = totals / lengths[None, :].astype(jnp.float32)
    owner = (dest_dp[n_sec - 1] == my_dp)[None, :] & (
        dest_slot[n_sec - 1][None, :] == jnp.arange(n_slots)[:, None]
    )
    sample_scores = jnp.sum(jnp.where(owner[:, None, :], averages[None, :, :], 0.0), axis=-1)
    return layer_out, sample_scores[None]


def solution(mesh):
    placed = (
        P(("sec", "dp"), "tp", None),
        P(),
        P(),
        P(),
        P("sec", None, "tp"),
        P("sec", None, None, "tp"),
        P("sec", "tp", None),
        P("sec", None),
        P("sec", None),
    )
    return jax.shard_map(
        on_device,
        mesh=mesh,
        in_specs=placed,
        out_specs=(P("sec", "dp", "tp", None, None), P("dp", None, None)),
        check_vma=False,
    )
```

```python
import functools
import math

import jax
import jax.numpy as jnp
from jax import lax
from jax.experimental import pallas as pl
from jax.experimental.pallas import tpu as pltpu
from jax.sharding import PartitionSpec as P

HD = 128
NORM_EPS = 1e-05
ROPE_THETA = 500000.0
VMEM_BYTES = 40 * 1024 * 1024
CHUNKS = (1, 1, 2, 2, 2)


def params():
    return pltpu.CompilerParams(vmem_limit_bytes=VMEM_BYTES)


def swap(value, axis, size, step):
    return lax.ppermute(value, axis, [(j, j ^ step) for j in range(size)])


sync = lax.optimization_barrier


def shift(value, axis, size, step):
    return lax.ppermute(value, axis, [(j, (j + step) % size) for j in range(size)])


def attention_kernel(n_dp, n_tp, n_pieces, n_done, with_prior, *refs):
    x_refs, refs = refs[:n_pieces], refs[n_pieces:]
    gain_ref, cos_ref, sin_ref, mask_ref, wq_ref, wkv_ref = refs[:6]
    refs = refs[6:]
    normed, acc_q, acc_k, acc_v = refs[-4:]
    refs = list(refs[:-4])
    prior_ref = refs.pop(0) if with_prior else None
    out_ref = refs.pop(0) if with_prior else None
    kept_ref = refs.pop(0) if refs else None
    group, step = pl.program_id(0), pl.program_id(1)
    steps, rows, depth = normed.shape
    seq = mask_ref.shape[0]
    width = steps * depth

    @pl.when((group == 0) & (step == 0))
    def _():
        start = 0
        for x_ref in x_refs:
            size = min(16, x_ref.shape[0])

            def norm_rows(i, carry, x_ref=x_ref, start=start, size=size):
                x = x_ref[pl.ds(pl.multiple_of(i * size, size), size), :].astype(jnp.float32)
                inv = lax.rsqrt(jnp.sum(x * x, axis=-1, keepdims=True) * (1.0 / width) + NORM_EPS)
                y = (x * inv * gain_ref[...]).astype(jnp.bfloat16)
                to = pl.ds(pl.multiple_of(start + i * size, size), size)
                for j in range(steps):
                    normed[j, to, :] = y[:, j * depth : (j + 1) * depth]
                return carry

            lax.fori_loop(0, x_ref.shape[0] // size, norm_rows, 0)
            start += x_ref.shape[0]

    lhs = normed[step]
    part_q = jnp.dot(lhs, wq_ref[...], preferred_element_type=jnp.float32)
    part_k = jnp.dot(lhs, wkv_ref[0], preferred_element_type=jnp.float32)
    part_v = jnp.dot(lhs, wkv_ref[1], preferred_element_type=jnp.float32)

    @pl.when(step == 0)
    def _():
        acc_q[...] = part_q
        acc_k[...] = part_k
        acc_v[...] = part_v

    @pl.when(step > 0)
    def _():
        acc_q[...] += part_q
        acc_k[...] += part_k
        acc_v[...] += part_v

    @pl.when(step == steps - 1)
    def _():
        local = seq // n_tp
        q_width, kv_width = acc_q.shape[1], acc_k.shape[1]
        per_kv = q_width // kv_width

        def rope(v, first):
            at = slice(first, first + v.shape[0])
            return (v * cos_ref[at] + pltpu.roll(v, HD // 2, 1) * sin_ref[at]).astype(jnp.bfloat16)

        if kept_ref is not None:
            for start in range(n_done, rows, local):
                at, to = slice(start, start + local), slice(start - n_done, start - n_done + local)
                for c in range(0, q_width, HD):
                    kept_ref[to, c : c + HD] = rope(acc_q[at, c : c + HD], 0)
                for c in range(0, kv_width, HD):
                    kept_ref[to, q_width + c : q_width + c + HD] = rope(acc_k[at, c : c + HD], 0)
                kept_ref[to, q_width + kv_width :] = acc_v[at].astype(jnp.bfloat16)

        if out_ref is not None:
            causal = jnp.concatenate([mask_ref[...]] * per_kv, axis=0) > 0.0
            block = seq // (n_dp * n_tp)
            more = seq - local
            for s in range(n_done // more):
                old, new = slice(s * local, (s + 1) * local), slice(s * more, (s + 1) * more)
                for j in range(kv_width // HD):
                    cols = slice(j * HD, (j + 1) * HD)
                    joined = lambda first, last: jnp.concatenate([first, last], axis=0)
                    kept = lambda start: prior_ref[old, start : start + HD]
                    keys = joined(kept(q_width + j * HD), rope(acc_k[new, cols], local))
                    values = joined(kept(q_width + kv_width + j * HD), acc_v[new, cols].astype(jnp.bfloat16))
                    heads = range(j * per_kv, (j + 1) * per_kv)
                    queries = [joined(kept(h * HD), rope(acc_q[new, h * HD : (h + 1) * HD], local)) for h in heads]
                    queries = jnp.concatenate(queries, axis=0)
                    scores = lax.dot_general(
                        queries, keys, (((1,), (1,)), ((), ())), preferred_element_type=jnp.float32
                    ) * (1.0 / math.sqrt(HD))
                    scores = jnp.where(causal, scores, -1e30)
                    expo = jnp.exp(scores - jnp.max(scores, axis=-1, keepdims=True))
                    weights = (expo / jnp.sum(expo, axis=-1, keepdims=True)).astype(jnp.bfloat16)
                    context = jnp.dot(weights, values, preferred_element_type=jnp.float32).astype(jnp.bfloat16)
                    for n, h in enumerate(heads):
                        for t in range(n_tp):
                            for z in range(n_dp):
                                start = n * seq + (t * n_dp + z) * block
                                out_ref[z, t, s, :, h * HD : (h + 1) * HD] = context[start : start + block]


def attention(pieces, prior, n_done, gain, cos, sin, mask, wq, wkv, n_dp, n_tp):
    rows, width = sum(p.shape[0] for p in pieces), pieces[0].shape[1]
    seq = mask.shape[0]
    q_width, kv_width = wq.shape[2], wkv.shape[3]
    kv_block = min(2 * HD, kv_width)
    groups = kv_width // kv_block
    q_block = q_width // groups
    steps = 2
    depth = width // steps
    samples = n_done // (seq - seq // n_tp)
    block = seq // (n_dp * n_tp)
    packed = q_block + 2 * kv_block
    fixed = lambda g, k: (0, 0)
    in_specs = [pl.BlockSpec(p.shape, fixed, pipeline_mode=pl.Buffered(1)) for p in pieces] + [
        pl.BlockSpec((1, width), fixed),
        pl.BlockSpec((seq, HD), fixed),
        pl.BlockSpec((seq, HD), fixed),
        pl.BlockSpec((seq, seq), fixed),
        pl.BlockSpec((None, depth, q_block), lambda g, k: (0, k, g)),
        pl.BlockSpec((None, 2, depth, kv_block), lambda g, k: (0, 0, k, g)),
    ]
    operands = [*pieces, gain, cos, sin, mask, wq, wkv]
    out_shape, out_specs = [], []
    if prior is not None:
        operands.append(prior)
        in_specs.append(pl.BlockSpec((None, prior.shape[1], packed), lambda g, k: (g, 0, 0)))
        out_shape.append(jax.ShapeDtypeStruct((n_dp, n_tp, samples, block, q_width), jnp.bfloat16))
        out_specs.append(pl.BlockSpec((n_dp, n_tp, samples, block, q_block), lambda g, k: (0, 0, 0, 0, g)))
    if n_done < rows:
        out_shape.append(jax.ShapeDtypeStruct((groups, rows - n_done, packed), jnp.bfloat16))
        out_specs.append(pl.BlockSpec((None, rows - n_done, packed), lambda g, k: (g, 0, 0)))
    return pl.pallas_call(
        functools.partial(attention_kernel, n_dp, n_tp, len(pieces), n_done, prior is not None),
        out_shape=out_shape,
        grid=(groups, steps),
        in_specs=in_specs,
        out_specs=out_specs,
        scratch_shapes=[
            pltpu.VMEM((steps, rows, depth), jnp.bfloat16),
            pltpu.VMEM((rows, q_block), jnp.float32),
            pltpu.VMEM((rows, kv_block), jnp.float32),
            pltpu.VMEM((rows, kv_block), jnp.float32),
        ],
        compiler_params=params(),
        cost_estimate=pl.CostEstimate(flops=1, bytes_accessed=1, transcendentals=0),
        name="project_and_attend",
    )(*operands)


def out_kernel(ctx_ref, wo_ref, own_ref, send_ref):
    full = jnp.dot(ctx_ref[...], wo_ref[...], preferred_element_type=jnp.float32).astype(jnp.bfloat16)
    mine = own_ref.shape[0]
    own_ref[...] = full[:mine]
    send_ref[...] = full[mine:]


def out_projection(ctx, wo, mine, first, cols):
    rows, depth = ctx.shape
    col_block = min(512, cols)
    inner = cols // col_block
    base = first // col_block
    return pl.pallas_call(
        out_kernel,
        out_shape=[
            jax.ShapeDtypeStruct((mine, cols), jnp.bfloat16),
            jax.ShapeDtypeStruct((rows - mine, cols), jnp.bfloat16),
        ],
        grid=(inner,),
        in_specs=[
            pl.BlockSpec((rows, depth), lambda n: (0, 0)),
            pl.BlockSpec((None, depth, col_block), lambda n: (0, 0, base + n)),
        ],
        out_specs=[
            pl.BlockSpec((mine, col_block), lambda n: (0, n)),
            pl.BlockSpec((rows - mine, col_block), lambda n: (0, n)),
        ],
        compiler_params=params(),
        cost_estimate=pl.CostEstimate(flops=1, bytes_accessed=1, transcendentals=0),
        name="out_projection",
    )(ctx, wo)


def join_kernel(n_slots, block, table_ref, near_ref, far_ref, near_other, far_other, resid_ref, pair_ref, head_ref, *out_refs):
    packed_refs, stats_ref = out_refs[:-1], out_refs[-1]
    head = head_ref[...]
    lane = lax.broadcasted_iota(jnp.int32, (block, HD), 1)
    row = lax.broadcasted_iota(jnp.int32, (block, 1), 0)
    step = pl.program_id(0)
    slots = packed_refs[0].shape[0]

    for dest, packed_ref in enumerate(packed_refs):
        for slot in range(slots):
            entry = dest * n_slots + step * slots + slot
            part, resid, live = table_ref[0, entry], table_ref[1, entry], table_ref[2, entry]
            is_far = table_ref[4, entry] > 0
            added = jnp.where(is_far, far_ref[part], near_ref[part]).astype(jnp.float32)
            for k in range(near_other.shape[0]):
                added = added + jnp.where(is_far, far_other[k, part], near_other[k, part]).astype(jnp.float32)
            rows_in = jnp.where(table_ref[3, entry] > 0, pair_ref[resid], resid_ref[resid])
            hidden = rows_in.astype(jnp.float32) + added
            packed_ref[slot] = jnp.where(row < live, hidden, 0.0).astype(jnp.bfloat16)
            squares = jnp.sum(hidden * hidden, axis=-1, keepdims=True)
            scored = jnp.sum(hidden * head, axis=-1, keepdims=True)
            stats_ref[dest, slot] = jnp.where(lane == 0, squares, jnp.where(lane == 1, scored, 0.0))


def join(table, owns, others, resid, resid_pair, head, chunk, n_dp, n_slots, block):
    cols = owns[0].shape[-1]
    slots = n_slots // 2
    fixed = lambda i, t: (0, 0, 0)
    here = lambda i, t: (0, 0, chunk)
    out = pl.pallas_call(
        functools.partial(join_kernel, n_slots, block),
        out_shape=[jax.ShapeDtypeStruct((n_slots, block, cols), jnp.bfloat16) for _ in range(n_dp)]
        + [jax.ShapeDtypeStruct((n_dp, n_slots, block, HD), jnp.float32)],
        grid_spec=pltpu.PrefetchScalarGridSpec(
            num_scalar_prefetch=1,
            grid=(n_slots // slots,),
            in_specs=[
                pl.BlockSpec(owns[0].shape, fixed),
                pl.BlockSpec(owns[1].shape, fixed),
                pl.BlockSpec(others[0].shape, lambda i, t: (0, 0, 0, 0)),
                pl.BlockSpec(others[1].shape, lambda i, t: (0, 0, 0, 0)),
                pl.BlockSpec((resid.shape[0], block, cols), here),
                pl.BlockSpec((resid.shape[0], block, cols), here),
                pl.BlockSpec((1, cols), lambda i, t: (0, chunk)),
            ],
            out_specs=[pl.BlockSpec((slots, block, cols), lambda i, t: (i, 0, 0)) for _ in range(n_dp)]
            + [pl.BlockSpec((n_dp, slots, block, HD), lambda i, t: (0, i, 0, 0))],
        ),
        compiler_params=params(),
        cost_estimate=pl.CostEstimate(flops=1, bytes_accessed=1, transcendentals=0),
        name="join_partials",
    )(table, *owns, *others, resid, resid_pair, head)
    return list(out[:-1]), out[-1]


def place_kernel(count, order_ref, *refs):
    out_ref = refs[-1]
    for k in range(count):
        out_ref[:, order_ref[k]] = refs[k][...]


def place(order, pieces, whole, chunk, width):
    n_slots, block, cols = pieces[0].shape
    count = len(pieces)
    rows = n_slots // 3
    specs = [pl.BlockSpec((rows, block, cols), lambda i, o: (i, 0, 0)) for _ in pieces]
    operands = list(pieces)
    aliases = {}
    if whole is not None:
        specs.append(pl.BlockSpec(memory_space=pl.ANY))
        operands.append(whole)
        aliases = {1 + count: 0}
    return pl.pallas_call(
        functools.partial(place_kernel, count),
        out_shape=jax.ShapeDtypeStruct((n_slots, count, block, width), jnp.bfloat16),
        grid_spec=pltpu.PrefetchScalarGridSpec(
            num_scalar_prefetch=1,
            grid=(n_slots // rows,),
            in_specs=specs,
            out_specs=pl.BlockSpec((rows, count, block, cols), lambda i, o: (i, 0, 0, chunk)),
        ),
        input_output_aliases=aliases,
        compiler_params=params(),
        cost_estimate=pl.CostEstimate(flops=1, bytes_accessed=1, transcendentals=0),
        name="place_rows",
    )(order, *operands)


def on_device(responses, lengths, dest_dp, dest_slot, wq, wkv, wo, norm_gain, head_vec):
    n_sec = lax.axis_size("sec")
    n_dp = lax.axis_size("dp")
    n_tp = lax.axis_size("tp")
    _, local_len, width = responses.shape
    samples = lengths.shape[0]
    n_slots = 3 * samples // (2 * n_dp)
    seq = local_len * n_tp
    block = local_len // n_dp
    my_sec, my_dp, my_tp = lax.axis_index("sec"), lax.axis_index("dp"), lax.axis_index("tp")

    owners = lax.rem(my_tp - jnp.arange(n_tp) + n_tp, n_tp)
    positions = (owners[:, None] * local_len + jnp.arange(local_len)[None, :]).reshape(seq)
    frequency = jnp.exp(jnp.arange(HD // 2, dtype=jnp.float32) * (-2.0 * math.log(ROPE_THETA) / HD))
    angles = positions.astype(jnp.float32)[:, None] * frequency[None, :]
    cos = jnp.tile(jnp.cos(angles), (1, 2))
    sin = jnp.concatenate([-jnp.sin(angles), jnp.sin(angles)], axis=1)
    mask = (positions[:, None] >= positions[None, :]).astype(jnp.float32)

    attend = lambda pieces, prior, n_done: attention(
        pieces, prior, n_done, norm_gain, cos, sin, mask, wq, wkv, n_dp, n_tp
    )

    def spread(ctx, steps):
        here = lambda k: lax.dynamic_index_in_dim(ctx, my_dp ^ k, 0, keepdims=False)
        return [swap(here(k), "dp", n_dp, k) if k else here(k) for k in steps]

    def gathered(parts):
        return jnp.stack(parts, axis=1).reshape(-1, wq.shape[2])

    mine = responses[0]
    near = [shift(mine, "tp", n_tp, k) for k in range(1, n_tp)]
    far_mine = swap(mine, "sec", n_sec, 2)
    mine_pair = swap(mine, "sec", n_sec, 1)
    mine, mine_pair, cos, sin, mask = sync((mine, mine_pair, cos, sin, mask))
    quarter = lambda k: lax.dynamic_slice_in_dim(mine, (my_dp ^ k) * block, block, 0)
    resid = [quarter(0)] + [swap(quarter(k), "dp", n_dp, k) for k in range(1, n_dp)]
    (kept,) = attend([mine, mine_pair], None, 0)
    near, far_mine, resid, kept = sync((near, far_mine, resid, kept))

    half = local_len // 2
    far = []
    for k in range(1, n_tp):
        parts = [shift(far_mine[:half], "tp", n_tp, k), swap(near[k - 1][half:], "sec", n_sec, 2)]
        far += parts if half % 16 == 0 else [jnp.concatenate(parts, axis=0)]
    near_pair = [swap(v, "sec", n_sec, 1) for v in near]
    far_mine_pair = swap(far_mine, "sec", n_sec, 1)
    near, near_pair, far_mine, far_mine_pair, kept, resid = sync(
        (near, near_pair, far_mine, far_mine_pair, kept, resid)
    )

    more = 2 * (seq - local_len)
    resid = jnp.stack(resid)
    resid_far = swap(resid, "sec", n_sec, 2)
    near_ctx, kept = attend(near + near_pair + [far_mine, far_mine_pair], kept, more)
    near_ctx, kept, far, resid, resid_far = sync((near_ctx, kept, far, resid, resid_far))

    near_rows = spread(near_ctx, range(n_dp))
    far_pair = [swap(v, "sec", n_sec, 1) for v in far]
    far, far_pair, kept = sync((far, far_pair, kept))
    (far_ctx,) = attend(far + far_pair, kept, more)
    near_rows, far_ctx, resid, resid_far = sync((near_rows, far_ctx, resid, resid_far))

    row_dp = lax.dynamic_index_in_dim(dest_dp, my_sec, 0, keepdims=False)
    row_slot = lax.dynamic_index_in_dim(dest_slot, my_sec, 0, keepdims=False)
    sample = jnp.arange(samples)
    i_rel = my_sec ^ (sample // n_dp)
    k_rel = my_dp ^ (sample % n_dp)
    part_at = k_rel * 2 + i_rel % 2
    resid_at = (i_rel // 2) * n_dp + k_rel
    dests = my_dp ^ jnp.arange(n_dp)
    chosen = (row_dp[None, None, :] == dests[:, None, None]) & (
        row_slot[None, None, :] == jnp.arange(n_slots)[None, :, None]
    )
    first_pos = my_tp * local_len + my_dp * block
    live = jnp.clip(lengths - first_pos, 0, block)
    pick = lambda v: jnp.sum(jnp.where(chosen, v[None, None, :], 0), axis=-1).reshape(-1)
    table = jnp.stack([pick(part_at), pick(resid_at), pick(live), pick(i_rel % 2), pick(i_rel // 2)]).astype(jnp.int32)
    order = dests.astype(jnp.int32)

    unit = width // sum(CHUNKS)
    starts = [unit * sum(CHUNKS[:c]) for c in range(len(CHUNKS))]
    count = len(CHUNKS)

    def project(chunk, ctx_rows):
        owned = ctx_rows.shape[0] // n_tp
        own, send = out_projection(ctx_rows, wo, owned, starts[chunk], unit * CHUNKS[chunk])
        own = own.reshape(-1, block, own.shape[-1])
        return own, send.reshape(n_tp - 1, -1, block, own.shape[-1])

    def exchange(projected):
        send = projected[1]
        return jnp.stack([shift(send[k - 1], "tp", n_tp, n_tp - k) for k in range(1, n_tp)])

    def finish(chunk, owns, others):
        return join(
            table, owns, others, resid, resid_pair, head_vec, starts[chunk] // (unit * CHUNKS[chunk]),
            n_dp, n_slots, block,
        )

    def put(whole, chunk, pieces):
        return place(order, pieces, whole, starts[chunk] // (unit * CHUNKS[chunk]), width)

    far_across = spread(far_ctx, range(n_dp // 2, n_dp // 2 + 1))
    near_rows = gathered(near_rows)
    near_projected = [project(c, near_rows) for c in range(2)]
    resid = jnp.concatenate([resid, resid_far], axis=0)
    far_across, near_projected, near_rows, far_ctx, resid = sync(
        (far_across, near_projected, near_rows, far_ctx, resid)
    )
    others = [k for k in range(n_dp) if k != n_dp // 2]
    far_rows = spread(far_ctx, others)
    far_rows.insert(n_dp // 2, far_across[0])
    near_others = [exchange(p) for p in near_projected]
    resid_pair = swap(resid, "sec", n_sec, 1)
    near_projected += [project(c, near_rows) for c in range(2, count - 1)]
    far_rows, near_others, near_projected, near_rows, resid_pair = sync(
        (far_rows, near_others, near_projected, near_rows, resid_pair)
    )

    far_rows = gathered(far_rows)
    first = project(0, far_rows)
    first, far_rows = sync((first, far_rows))
    far_others = [exchange(first)]
    far_projected = [first, project(1, far_rows)]
    far_others, far_projected, far_rows = sync((far_others, far_projected, far_rows))
    packed, part = finish(0, [near_projected[0][0], first[0]], [near_others[0], far_others[0]])
    packed, far_projected, far_rows = sync((packed, far_projected, far_rows))

    stats, whole, pieces = [part], None, None
    for chunk in range(count):
        moved = [packed[0]] + [swap(packed[k], "dp", n_dp, k) for k in range(1, n_dp)]
        if pieces is not None:
            whole = put(whole, chunk - 1, pieces)
        ahead = chunk + 1
        if ahead < count:
            far_others.append(exchange(far_projected[ahead]))
            if len(near_others) == ahead:
                near_others.append(exchange(near_projected[ahead]))
            elif ahead + 1 < count - 1:
                near_others.append(exchange(near_projected[ahead + 1]))
            if ahead + 1 < count:
                far_projected.append(project(ahead + 1, far_rows))
                if ahead + 1 == count - 1:
                    near_projected.append(project(ahead + 1, near_rows))
            owns = [near_projected[ahead][0], far_projected[ahead][0]]
            packed, part = finish(ahead, owns, [near_others[ahead], far_others[ahead]])
            stats.append(part)
            moved, packed, whole, far_rows, far_projected, near_others[-1] = sync(
                (moved, packed, whole, far_rows, far_projected, near_others[-1])
            )
        pieces = moved
    whole = put(whole, count - 1, pieces)
    layer_out = jnp.transpose(whole.reshape(n_slots, local_len, width), (1, 0, 2))[None, None]

    stats = sum(v[..., :2] for v in stats)
    token_scores = stats[..., 1] * lax.rsqrt(stats[..., 0] * (1.0 / width) + NORM_EPS)
    is_live = jnp.arange(block)[None, None, :] < table[2].reshape(n_dp, n_slots, 1)
    slot_sums = jnp.sum(jnp.where(is_live, token_scores, 0.0), axis=-1)
    by_sample = jnp.sum(jnp.where(chosen, slot_sums[:, :, None], 0.0), axis=(0, 1))
    by_model = jnp.where(jnp.arange(n_sec)[:, None] == my_sec, by_sample[None, :], 0.0)
    for axis, size in (("tp", n_tp), ("dp", n_dp), ("sec", n_sec)):
        by_model = sum([shift(by_model, axis, size, k) for k in range(1, size)], by_model)
    totals = by_model
    averages = totals / lengths[None, :].astype(jnp.float32)
    owner = (dest_dp[n_sec - 1] == my_dp)[None, :] & (
        dest_slot[n_sec - 1][None, :] == jnp.arange(n_slots)[:, None]
    )
    sample_scores = jnp.sum(jnp.where(owner[:, None, :], averages[None, :, :], 0.0), axis=-1)
    return layer_out, sample_scores[None]


def solution(mesh):
    placed = (
        P(("sec", "dp"), "tp", None),
        P(),
        P(),
        P(),
        P("sec", None, "tp"),
        P("sec", None, None, "tp"),
        P("sec", "tp", None),
        P("sec", None),
        P("sec", None),
    )
    return jax.shard_map(
        on_device,
        mesh=mesh,
        in_specs=placed,
        out_specs=(P("sec", "dp", "tp", None, None), P("dp", None, None)),
        check_vma=False,
    )
```

```python
import functools
import math

import jax
import jax.numpy as jnp
from jax import lax
from jax.experimental import pallas as pl
from jax.experimental.pallas import tpu as pltpu
from jax.sharding import PartitionSpec as P

HD = 128
NORM_EPS = 1e-05
ROPE_THETA = 500000.0
VMEM_BYTES = 40 * 1024 * 1024
CHUNKS = (1, 1, 2, 2, 2)
SPLIT = 3


def params():
    return pltpu.CompilerParams(vmem_limit_bytes=VMEM_BYTES)


def swap(value, axis, size, step):
    return lax.ppermute(value, axis, [(j, j ^ step) for j in range(size)])


sync = lax.optimization_barrier


def shift(value, axis, size, step):
    return lax.ppermute(value, axis, [(j, (j + step) % size) for j in range(size)])


def attention_kernel(n_dp, n_tp, n_pieces, n_done, with_prior, *refs):
    x_refs, refs = refs[:n_pieces], refs[n_pieces:]
    gain_ref, cos_ref, sin_ref, mask_ref, wq_ref, wkv_ref = refs[:6]
    refs = refs[6:]
    normed, acc_q, acc_k, acc_v = refs[-4:]
    refs = list(refs[:-4])
    prior_ref = refs.pop(0) if with_prior else None
    out_ref = refs.pop(0) if with_prior else None
    kept_ref = refs.pop(0) if refs else None
    group, step = pl.program_id(0), pl.program_id(1)
    steps, rows, depth = normed.shape
    seq = mask_ref.shape[0]
    width = steps * depth

    @pl.when((group == 0) & (step == 0))
    def _():
        start = 0
        for x_ref in x_refs:
            size = min(16, x_ref.shape[0])

            def norm_rows(i, carry, x_ref=x_ref, start=start, size=size):
                x = x_ref[pl.ds(pl.multiple_of(i * size, size), size), :].astype(jnp.float32)
                inv = lax.rsqrt(jnp.sum(x * x, axis=-1, keepdims=True) * (1.0 / width) + NORM_EPS)
                y = (x * inv * gain_ref[...]).astype(jnp.bfloat16)
                to = pl.ds(pl.multiple_of(start + i * size, size), size)
                for j in range(steps):
                    normed[j, to, :] = y[:, j * depth : (j + 1) * depth]
                return carry

            lax.fori_loop(0, x_ref.shape[0] // size, norm_rows, 0)
            start += x_ref.shape[0]

    lhs = normed[step]
    part_q = jnp.dot(lhs, wq_ref[...], preferred_element_type=jnp.float32)
    part_k = jnp.dot(lhs, wkv_ref[0], preferred_element_type=jnp.float32)
    part_v = jnp.dot(lhs, wkv_ref[1], preferred_element_type=jnp.float32)

    @pl.when(step == 0)
    def _():
        acc_q[...] = part_q
        acc_k[...] = part_k
        acc_v[...] = part_v

    @pl.when(step > 0)
    def _():
        acc_q[...] += part_q
        acc_k[...] += part_k
        acc_v[...] += part_v

    @pl.when(step == steps - 1)
    def _():
        local = seq // n_tp
        q_width, kv_width = acc_q.shape[1], acc_k.shape[1]
        per_kv = q_width // kv_width

        def rope(v, first):
            at = slice(first, first + v.shape[0])
            return (v * cos_ref[at] + pltpu.roll(v, HD // 2, 1) * sin_ref[at]).astype(jnp.bfloat16)

        if kept_ref is not None:
            for start in range(n_done, rows, local):
                at, to = slice(start, start + local), slice(start - n_done, start - n_done + local)
                for c in range(0, q_width, HD):
                    kept_ref[to, c : c + HD] = rope(acc_q[at, c : c + HD], 0)
                for c in range(0, kv_width, HD):
                    kept_ref[to, q_width + c : q_width + c + HD] = rope(acc_k[at, c : c + HD], 0)
                kept_ref[to, q_width + kv_width :] = acc_v[at].astype(jnp.bfloat16)

        if out_ref is not None:
            causal = jnp.concatenate([mask_ref[...]] * per_kv, axis=0) > 0.0
            block = seq // (n_dp * n_tp)
            more = seq - local
            for s in range(n_done // more):
                old, new = slice(s * local, (s + 1) * local), slice(s * more, (s + 1) * more)
                for j in range(kv_width // HD):
                    cols = slice(j * HD, (j + 1) * HD)
                    joined = lambda first, last: jnp.concatenate([first, last], axis=0)
                    kept = lambda start: prior_ref[old, start : start + HD]
                    keys = joined(kept(q_width + j * HD), rope(acc_k[new, cols], local))
                    values = joined(kept(q_width + kv_width + j * HD), acc_v[new, cols].astype(jnp.bfloat16))
                    heads = range(j * per_kv, (j + 1) * per_kv)
                    queries = [joined(kept(h * HD), rope(acc_q[new, h * HD : (h + 1) * HD], local)) for h in heads]
                    queries = jnp.concatenate(queries, axis=0)
                    scores = lax.dot_general(
                        queries, keys, (((1,), (1,)), ((), ())), preferred_element_type=jnp.float32
                    ) * (1.0 / math.sqrt(HD))
                    scores = jnp.where(causal, scores, -1e30)
                    expo = jnp.exp(scores - jnp.max(scores, axis=-1, keepdims=True))
                    weights = (expo / jnp.sum(expo, axis=-1, keepdims=True)).astype(jnp.bfloat16)
                    context = jnp.dot(weights, values, preferred_element_type=jnp.float32).astype(jnp.bfloat16)
                    for n, h in enumerate(heads):
                        for t in range(n_tp):
                            for z in range(n_dp):
                                start = n * seq + (t * n_dp + z) * block
                                out_ref[z, t, s, :, h * HD : (h + 1) * HD] = context[start : start + block]


def attention(pieces, prior, n_done, gain, cos, sin, mask, wq, wkv, n_dp, n_tp):
    rows, width = sum(p.shape[0] for p in pieces), pieces[0].shape[1]
    seq = mask.shape[0]
    q_width, kv_width = wq.shape[2], wkv.shape[3]
    kv_block = min(2 * HD, kv_width)
    groups = kv_width // kv_block
    q_block = q_width // groups
    steps = 2
    depth = width // steps
    samples = n_done // (seq - seq // n_tp)
    block = seq // (n_dp * n_tp)
    packed = q_block + 2 * kv_block
    fixed = lambda g, k: (0, 0)
    in_specs = [pl.BlockSpec(p.shape, fixed, pipeline_mode=pl.Buffered(1)) for p in pieces] + [
        pl.BlockSpec((1, width), fixed),
        pl.BlockSpec((seq, HD), fixed),
        pl.BlockSpec((seq, HD), fixed),
        pl.BlockSpec((seq, seq), fixed),
        pl.BlockSpec((None, depth, q_block), lambda g, k: (0, k, g)),
        pl.BlockSpec((None, 2, depth, kv_block), lambda g, k: (0, 0, k, g)),
    ]
    operands = [*pieces, gain, cos, sin, mask, wq, wkv]
    out_shape, out_specs = [], []
    if prior is not None:
        operands.append(prior)
        in_specs.append(pl.BlockSpec((None, prior.shape[1], packed), lambda g, k: (g, 0, 0)))
        out_shape.append(jax.ShapeDtypeStruct((n_dp, n_tp, samples, block, q_width), jnp.bfloat16))
        out_specs.append(pl.BlockSpec((n_dp, n_tp, samples, block, q_block), lambda g, k: (0, 0, 0, 0, g)))
    if n_done < rows:
        out_shape.append(jax.ShapeDtypeStruct((groups, rows - n_done, packed), jnp.bfloat16))
        out_specs.append(pl.BlockSpec((None, rows - n_done, packed), lambda g, k: (g, 0, 0)))
    return pl.pallas_call(
        functools.partial(attention_kernel, n_dp, n_tp, len(pieces), n_done, prior is not None),
        out_shape=out_shape,
        grid=(groups, steps),
        in_specs=in_specs,
        out_specs=out_specs,
        scratch_shapes=[
            pltpu.VMEM((steps, rows, depth), jnp.bfloat16),
            pltpu.VMEM((rows, q_block), jnp.float32),
            pltpu.VMEM((rows, kv_block), jnp.float32),
            pltpu.VMEM((rows, kv_block), jnp.float32),
        ],
        compiler_params=params(),
        cost_estimate=pl.CostEstimate(flops=1, bytes_accessed=1, transcendentals=0),
        name="project_and_attend",
    )(*operands)


def out_kernel(ctx_ref, wo_ref, own_ref, send_ref):
    full = jnp.dot(ctx_ref[...], wo_ref[...], preferred_element_type=jnp.float32).astype(jnp.bfloat16)
    mine = own_ref.shape[0]
    own_ref[...] = full[:mine]
    send_ref[...] = full[mine:]


def out_projection(ctx, wo, mine, first, cols):
    rows, depth = ctx.shape
    col_block = min(512, cols)
    inner = cols // col_block
    base = first // col_block
    return pl.pallas_call(
        out_kernel,
        out_shape=[
            jax.ShapeDtypeStruct((mine, cols), jnp.bfloat16),
            jax.ShapeDtypeStruct((rows - mine, cols), jnp.bfloat16),
        ],
        grid=(inner,),
        in_specs=[
            pl.BlockSpec((rows, depth), lambda n: (0, 0)),
            pl.BlockSpec((None, depth, col_block), lambda n: (0, 0, base + n)),
        ],
        out_specs=[
            pl.BlockSpec((mine, col_block), lambda n: (0, n)),
            pl.BlockSpec((rows - mine, col_block), lambda n: (0, n)),
        ],
        compiler_params=params(),
        cost_estimate=pl.CostEstimate(flops=1, bytes_accessed=1, transcendentals=0),
        name="out_projection",
    )(ctx, wo)


def join_kernel(n_slots, block, table_ref, near_ref, far_ref, near_other, far_other, resid_ref, pair_ref, head_ref, *out_refs):
    packed_refs, stats_ref = out_refs[:-1], out_refs[-1]
    head = head_ref[...]
    lane = lax.broadcasted_iota(jnp.int32, (block, HD), 1)
    row = lax.broadcasted_iota(jnp.int32, (block, 1), 0)
    step = pl.program_id(0)
    slots = packed_refs[0].shape[0]

    for dest, packed_ref in enumerate(packed_refs):
        for slot in range(slots):
            entry = dest * n_slots + step * slots + slot
            part, resid, live = table_ref[0, entry], table_ref[1, entry], table_ref[2, entry]
            is_far = table_ref[4, entry] > 0
            added = jnp.where(is_far, far_ref[part], near_ref[part]).astype(jnp.float32)
            for k in range(near_other.shape[0]):
                added = added + jnp.where(is_far, far_other[k, part], near_other[k, part]).astype(jnp.float32)
            rows_in = jnp.where(table_ref[3, entry] > 0, pair_ref[resid], resid_ref[resid])
            hidden = rows_in.astype(jnp.float32) + added
            packed_ref[slot] = jnp.where(row < live, hidden, 0.0).astype(jnp.bfloat16)
            squares = jnp.sum(hidden * hidden, axis=-1, keepdims=True)
            scored = jnp.sum(hidden * head, axis=-1, keepdims=True)
            stats_ref[dest, slot] = jnp.where(lane == 0, squares, jnp.where(lane == 1, scored, 0.0))


def join(table, owns, others, resid, resid_pair, head, chunk, n_dp, n_slots, block):
    cols = owns[0][0].shape[-1]
    blocks = resid.shape[0]
    slots = n_slots // 2
    fixed = lambda i, t: (0, 0, 0)
    here = lambda i, t: (0, 0, chunk)
    out = pl.pallas_call(
        functools.partial(join_kernel, n_slots, block),
        out_shape=[jax.ShapeDtypeStruct((n_slots, block, cols), jnp.bfloat16) for _ in range(n_dp)]
        + [jax.ShapeDtypeStruct((n_dp, n_slots, block, HD), jnp.float32)],
        grid_spec=pltpu.PrefetchScalarGridSpec(
            num_scalar_prefetch=1,
            grid=(n_slots // slots,),
            in_specs=[
                *[pl.BlockSpec((blocks, block, cols), lambda i, t, at=at: (at, 0, 0)) for _, at in owns],
                *[pl.BlockSpec((v.shape[0], blocks, block, cols), lambda i, t, at=at: (0, at, 0, 0)) for v, at in others],
                pl.BlockSpec((resid.shape[0], block, cols), here),
                pl.BlockSpec((resid.shape[0], block, cols), here),
                pl.BlockSpec((1, cols), lambda i, t: (0, chunk)),
            ],
            out_specs=[pl.BlockSpec((slots, block, cols), lambda i, t: (i, 0, 0)) for _ in range(n_dp)]
            + [pl.BlockSpec((n_dp, slots, block, HD), lambda i, t: (0, i, 0, 0))],
        ),
        compiler_params=params(),
        cost_estimate=pl.CostEstimate(flops=1, bytes_accessed=1, transcendentals=0),
        name="join_partials",
    )(table, *[v for v, _ in owns], *[v for v, _ in others], resid, resid_pair, head)
    return list(out[:-1]), out[-1]


def place_kernel(count, order_ref, *refs):
    out_ref = refs[-1]
    for k in range(count):
        out_ref[:, order_ref[k]] = refs[k][...]


def place(order, pieces, whole, chunk, width):
    n_slots, block, cols = pieces[0].shape
    count = len(pieces)
    rows = n_slots // 3
    specs = [pl.BlockSpec((rows, block, cols), lambda i, o: (i, 0, 0)) for _ in pieces]
    operands = list(pieces)
    aliases = {}
    if whole is not None:
        specs.append(pl.BlockSpec(memory_space=pl.ANY))
        operands.append(whole)
        aliases = {1 + count: 0}
    return pl.pallas_call(
        functools.partial(place_kernel, count),
        out_shape=jax.ShapeDtypeStruct((n_slots, count, block, width), jnp.bfloat16),
        grid_spec=pltpu.PrefetchScalarGridSpec(
            num_scalar_prefetch=1,
            grid=(n_slots // rows,),
            in_specs=specs,
            out_specs=pl.BlockSpec((rows, count, block, cols), lambda i, o: (i, 0, 0, chunk)),
        ),
        input_output_aliases=aliases,
        compiler_params=params(),
        cost_estimate=pl.CostEstimate(flops=1, bytes_accessed=1, transcendentals=0),
        name="place_rows",
    )(order, *operands)


def on_device(responses, lengths, dest_dp, dest_slot, wq, wkv, wo, norm_gain, head_vec):
    n_sec = lax.axis_size("sec")
    n_dp = lax.axis_size("dp")
    n_tp = lax.axis_size("tp")
    _, local_len, width = responses.shape
    samples = lengths.shape[0]
    n_slots = 3 * samples // (2 * n_dp)
    seq = local_len * n_tp
    block = local_len // n_dp
    my_sec, my_dp, my_tp = lax.axis_index("sec"), lax.axis_index("dp"), lax.axis_index("tp")

    owners = lax.rem(my_tp - jnp.arange(n_tp) + n_tp, n_tp)
    positions = (owners[:, None] * local_len + jnp.arange(local_len)[None, :]).reshape(seq)
    frequency = jnp.exp(jnp.arange(HD // 2, dtype=jnp.float32) * (-2.0 * math.log(ROPE_THETA) / HD))
    angles = positions.astype(jnp.float32)[:, None] * frequency[None, :]
    cos = jnp.tile(jnp.cos(angles), (1, 2))
    sin = jnp.concatenate([-jnp.sin(angles), jnp.sin(angles)], axis=1)
    mask = (positions[:, None] >= positions[None, :]).astype(jnp.float32)

    attend = lambda pieces, prior, n_done: attention(
        pieces, prior, n_done, norm_gain, cos, sin, mask, wq, wkv, n_dp, n_tp
    )

    def by_step(ctx):
        return [lax.dynamic_index_in_dim(ctx, my_dp ^ k, 0, keepdims=False) for k in range(n_dp)]

    def spread(parts):
        return [parts[0]] + [swap(parts[k], "dp", n_dp, k) for k in range(1, n_dp)]

    def gathered(parts):
        return jnp.stack(parts, axis=1).reshape(-1, wq.shape[2])

    mine = responses[0]
    near = [shift(mine, "tp", n_tp, k) for k in range(1, n_tp)]
    far_mine = swap(mine, "sec", n_sec, 2)
    mine_pair = swap(mine, "sec", n_sec, 1)
    mine, mine_pair, cos, sin, mask = sync((mine, mine_pair, cos, sin, mask))
    quarter = lambda k: lax.dynamic_slice_in_dim(mine, (my_dp ^ k) * block, block, 0)
    resid = [quarter(0)] + [swap(quarter(k), "dp", n_dp, k) for k in range(1, n_dp)]
    (kept,) = attend([mine, mine_pair], None, 0)
    near, far_mine, resid, kept = sync((near, far_mine, resid, kept))

    half = local_len // 2
    far = []
    for k in range(1, n_tp):
        parts = [shift(far_mine[:half], "tp", n_tp, k), swap(near[k - 1][half:], "sec", n_sec, 2)]
        far += parts if half % 16 == 0 else [jnp.concatenate(parts, axis=0)]
    near_pair = [swap(v, "sec", n_sec, 1) for v in near]
    far_mine_pair = swap(far_mine, "sec", n_sec, 1)
    resid = jnp.stack(resid)
    near, near_pair, far_mine, far_mine_pair, kept, resid = sync(
        (near, near_pair, far_mine, far_mine_pair, kept, resid)
    )

    more = 2 * (seq - local_len)
    near_ctx, kept = attend(near + near_pair + [far_mine, far_mine_pair], kept, more)
    near_ctx, kept, far = sync((near_ctx, kept, far))

    near_rows = spread(by_step(near_ctx))
    far_pair = [swap(v, "sec", n_sec, 1) for v in far]
    far, far_pair, kept, resid = sync((far, far_pair, kept, resid))
    resid_far = swap(resid, "sec", n_sec, 2)
    (far_ctx,) = attend(far + far_pair, kept, more)
    across = lax.dynamic_index_in_dim(far_ctx, my_dp ^ 2, 0, keepdims=False)
    near_rows, far_ctx, across = sync((near_rows, far_ctx, across))

    row_dp = lax.dynamic_index_in_dim(dest_dp, my_sec, 0, keepdims=False)
    row_slot = lax.dynamic_index_in_dim(dest_slot, my_sec, 0, keepdims=False)
    sample = jnp.arange(samples)
    i_rel = my_sec ^ (sample // n_dp)
    k_rel = my_dp ^ (sample % n_dp)
    part_at = k_rel * 2 + i_rel % 2
    resid_at = (i_rel // 2) * n_dp + k_rel
    dests = my_dp ^ jnp.arange(n_dp)
    chosen = (row_dp[None, None, :] == dests[:, None, None]) & (
        row_slot[None, None, :] == jnp.arange(n_slots)[None, :, None]
    )
    first_pos = my_tp * local_len + my_dp * block
    live = jnp.clip(lengths - first_pos, 0, block)
    pick = lambda v: jnp.sum(jnp.where(chosen, v[None, None, :], 0), axis=-1).reshape(-1)
    table = jnp.stack([pick(part_at), pick(resid_at), pick(live), pick(i_rel % 2), pick(i_rel // 2)]).astype(jnp.int32)
    order = dests.astype(jnp.int32)

    unit = width // sum(CHUNKS)
    starts = [unit * sum(CHUNKS[:c]) for c in range(len(CHUNKS))]
    count = len(CHUNKS)

    def project(chunk, ctx_rows):
        owned = ctx_rows.shape[0] // n_tp
        own, send = out_projection(ctx_rows, wo, owned, starts[chunk], unit * CHUNKS[chunk])
        own = own.reshape(-1, block, own.shape[-1])
        return own, send.reshape(n_tp - 1, -1, block, own.shape[-1])

    def exchange(projected):
        send = projected[1]
        return jnp.stack([shift(send[k - 1], "tp", n_tp, n_tp - k) for k in range(1, n_tp)])

    def finish(chunk, owns, others):
        return join(
            table, owns, others, resid, resid_pair, head_vec, starts[chunk] // (unit * CHUNKS[chunk]),
            n_dp, n_slots, block,
        )

    def put(whole, chunk, pieces):
        return place(order, pieces, whole, starts[chunk] // (unit * CHUNKS[chunk]), width)

    far_across = swap(across, "dp", n_dp, 2)
    far_rows, near_rows = by_step(far_ctx), gathered(near_rows)
    resid = jnp.concatenate([resid, resid_far], axis=0)
    far_rows, near_rows, resid = sync((far_rows, near_rows, resid))
    near_projected = [project(c, near_rows) for c in range(2)]
    far_rows, far_across, near_projected, near_rows, resid = sync(
        (far_rows, far_across, near_projected, near_rows, resid)
    )
    far_rows = [far_across if k == 2 else swap(v, "dp", n_dp, k) if k else v for k, v in enumerate(far_rows)]
    near_others = [exchange(p) for p in near_projected]
    resid_pair = swap(resid, "sec", n_sec, 1)
    near_projected += [project(c, near_rows) for c in range(2, SPLIT)]
    far_rows, near_others, near_projected, near_rows, resid_pair = sync(
        (far_rows, near_others, near_projected, near_rows, resid_pair)
    )

    far_rows = gathered(far_rows)
    far_projected = [project(0, far_rows)]
    far_projected, far_rows = sync((far_projected, far_rows))
    far_others = [exchange(far_projected[0])]
    far_projected.append(project(1, far_rows))
    far_others, far_projected, far_rows = sync((far_others, far_projected, far_rows))

    def halves(near, far):
        return [(near, 0), (far, 0)]

    packed, part = finish(
        0, halves(near_projected[0][0], far_projected[0][0]), halves(near_others[0], far_others[0])
    )
    packed, far_projected, far_rows = sync((packed, far_projected, far_rows))

    stats, whole, pieces, projected = [part], None, None, None
    all_rows = jnp.concatenate([v.reshape(n_tp, -1, v.shape[-1]) for v in (near_rows, far_rows)], axis=1)
    all_rows = all_rows.reshape(-1, wq.shape[2])
    for chunk in range(count):
        moved = [packed[0]] + [swap(packed[k], "dp", n_dp, k) for k in range(1, n_dp)]
        if pieces is not None:
            whole = put(whole, chunk - 1, pieces)
        ahead = chunk + 1
        if ahead < count:
            if ahead < SPLIT:
                owns = halves(near_projected[ahead][0], far_projected[ahead][0])
                others = halves(near_others[ahead], exchange(far_projected[ahead]))
            else:
                other = exchange(projected)
                owns, others = [(projected[0], 0), (projected[0], 1)], [(other, 0), (other, 1)]
            if ahead + 1 < SPLIT:
                near_others.append(exchange(near_projected[ahead + 1]))
                far_projected.append(project(ahead + 1, far_rows))
            elif ahead + 1 < count:
                projected = project(ahead + 1, all_rows)
            packed, part = finish(ahead, owns, others)
            stats.append(part)
            moved, packed, whole, all_rows, far_projected, near_others, projected = sync(
                (moved, packed, whole, all_rows, far_projected, near_others, projected)
            )
        pieces = moved
    whole = put(whole, count - 1, pieces)
    layer_out = jnp.transpose(whole.reshape(n_slots, local_len, width), (1, 0, 2))[None, None]

    stats = sum(v[..., :2] for v in stats)
    token_scores = stats[..., 1] * lax.rsqrt(stats[..., 0] * (1.0 / width) + NORM_EPS)
    is_live = jnp.arange(block)[None, None, :] < table[2].reshape(n_dp, n_slots, 1)
    slot_sums = jnp.sum(jnp.where(is_live, token_scores, 0.0), axis=-1)
    by_sample = jnp.sum(jnp.where(chosen, slot_sums[:, :, None], 0.0), axis=(0, 1))
    by_model = jnp.where(jnp.arange(n_sec)[:, None] == my_sec, by_sample[None, :], 0.0)
    for axis, size in (("tp", n_tp), ("dp", n_dp), ("sec", n_sec)):
        by_model = sum([shift(by_model, axis, size, k) for k in range(1, size)], by_model)
    totals = by_model
    averages = totals / lengths[None, :].astype(jnp.float32)
    owner = (dest_dp[n_sec - 1] == my_dp)[None, :] & (
        dest_slot[n_sec - 1][None, :] == jnp.arange(n_slots)[:, None]
    )
    sample_scores = jnp.sum(jnp.where(owner[:, None, :], averages[None, :, :], 0.0), axis=-1)
    return layer_out, sample_scores[None]


def solution(mesh):
    placed = (
        P(("sec", "dp"), "tp", None),
        P(),
        P(),
        P(),
        P("sec", None, "tp"),
        P("sec", None, None, "tp"),
        P("sec", "tp", None),
        P("sec", None),
        P("sec", None),
    )
    return jax.shard_map(
        on_device,
        mesh=mesh,
        in_specs=placed,
        out_specs=(P("sec", "dp", "tp", None, None), P("dp", None, None)),
        check_vma=False,
    )
```

```python
import functools
import math

import jax
import jax.numpy as jnp
from jax import lax
from jax.experimental import pallas as pl
from jax.experimental.pallas import tpu as pltpu
from jax.sharding import PartitionSpec as P

HD = 128
NORM_EPS = 1e-05
ROPE_THETA = 500000.0
VMEM_BYTES = 40 * 1024 * 1024
CHUNKS = (1, 1, 2, 2, 2)
SPLIT = 3


def params():
    return pltpu.CompilerParams(vmem_limit_bytes=VMEM_BYTES)


def swap(value, axis, size, step):
    return lax.ppermute(value, axis, [(j, j ^ step) for j in range(size)])


sync = lax.optimization_barrier


def shift(value, axis, size, step):
    return lax.ppermute(value, axis, [(j, (j + step) % size) for j in range(size)])


def attention_kernel(n_dp, n_tp, n_pieces, n_done, with_prior, *refs):
    x_refs, refs = refs[:n_pieces], refs[n_pieces:]
    gain_ref, cos_ref, sin_ref, mask_ref, wq_ref, wkv_ref = refs[:6]
    refs = refs[6:]
    normed, acc_q, acc_k, acc_v = refs[-4:]
    refs = list(refs[:-4])
    prior_ref = refs.pop(0) if with_prior else None
    out_ref = refs.pop(0) if with_prior else None
    kept_ref = refs.pop(0) if refs else None
    group, step = pl.program_id(0), pl.program_id(1)
    steps, rows, depth = normed.shape
    seq = mask_ref.shape[0]
    width = steps * depth

    @pl.when((group == 0) & (step == 0))
    def _():
        start = 0
        for x_ref in x_refs:
            size = min(16, x_ref.shape[0])

            def norm_rows(i, carry, x_ref=x_ref, start=start, size=size):
                x = x_ref[pl.ds(pl.multiple_of(i * size, size), size), :].astype(jnp.float32)
                inv = lax.rsqrt(jnp.sum(x * x, axis=-1, keepdims=True) * (1.0 / width) + NORM_EPS)
                y = (x * inv * gain_ref[...]).astype(jnp.bfloat16)
                to = pl.ds(pl.multiple_of(start + i * size, size), size)
                for j in range(steps):
                    normed[j, to, :] = y[:, j * depth : (j + 1) * depth]
                return carry

            lax.fori_loop(0, x_ref.shape[0] // size, norm_rows, 0)
            start += x_ref.shape[0]

    lhs = normed[step]
    part_q = jnp.dot(lhs, wq_ref[...], preferred_element_type=jnp.float32)
    part_k = jnp.dot(lhs, wkv_ref[0], preferred_element_type=jnp.float32)
    part_v = jnp.dot(lhs, wkv_ref[1], preferred_element_type=jnp.float32)

    @pl.when(step == 0)
    def _():
        acc_q[...] = part_q
        acc_k[...] = part_k
        acc_v[...] = part_v

    @pl.when(step > 0)
    def _():
        acc_q[...] += part_q
        acc_k[...] += part_k
        acc_v[...] += part_v

    @pl.when(step == steps - 1)
    def _():
        local = seq // n_tp
        q_width, kv_width = acc_q.shape[1], acc_k.shape[1]
        per_kv = q_width // kv_width

        def rope(v, first):
            at = slice(first, first + v.shape[0])
            return (v * cos_ref[at] + pltpu.roll(v, HD // 2, 1) * sin_ref[at]).astype(jnp.bfloat16)

        if kept_ref is not None:
            for start in range(n_done, rows, local):
                at, to = slice(start, start + local), slice(start - n_done, start - n_done + local)
                for c in range(0, q_width, HD):
                    kept_ref[to, c : c + HD] = rope(acc_q[at, c : c + HD], 0)
                for c in range(0, kv_width, HD):
                    kept_ref[to, q_width + c : q_width + c + HD] = rope(acc_k[at, c : c + HD], 0)
                kept_ref[to, q_width + kv_width :] = acc_v[at].astype(jnp.bfloat16)

        if out_ref is not None:
            causal = jnp.concatenate([mask_ref[...]] * per_kv, axis=0) > 0.0
            block = seq // (n_dp * n_tp)
            more = seq - local
            for s in range(n_done // more):
                old, new = slice(s * local, (s + 1) * local), slice(s * more, (s + 1) * more)
                for j in range(kv_width // HD):
                    cols = slice(j * HD, (j + 1) * HD)
                    joined = lambda first, last: jnp.concatenate([first, last], axis=0)
                    kept = lambda start: prior_ref[old, start : start + HD]
                    keys = joined(kept(q_width + j * HD), rope(acc_k[new, cols], local))
                    values = joined(kept(q_width + kv_width + j * HD), acc_v[new, cols].astype(jnp.bfloat16))
                    heads = range(j * per_kv, (j + 1) * per_kv)
                    queries = [joined(kept(h * HD), rope(acc_q[new, h * HD : (h + 1) * HD], local)) for h in heads]
                    queries = jnp.concatenate(queries, axis=0)
                    scores = lax.dot_general(
                        queries, keys, (((1,), (1,)), ((), ())), preferred_element_type=jnp.float32
                    ) * (1.0 / math.sqrt(HD))
                    scores = jnp.where(causal, scores, -1e30)
                    expo = jnp.exp(scores - jnp.max(scores, axis=-1, keepdims=True))
                    weights = (expo / jnp.sum(expo, axis=-1, keepdims=True)).astype(jnp.bfloat16)
                    context = jnp.dot(weights, values, preferred_element_type=jnp.float32).astype(jnp.bfloat16)
                    for n, h in enumerate(heads):
                        for t in range(n_tp):
                            for z in range(n_dp):
                                start = n * seq + (t * n_dp + z) * block
                                out_ref[z, t, s, :, h * HD : (h + 1) * HD] = context[start : start + block]


def attention(pieces, prior, n_done, gain, cos, sin, mask, wq, wkv, n_dp, n_tp):
    rows, width = sum(p.shape[0] for p in pieces), pieces[0].shape[1]
    seq = mask.shape[0]
    q_width, kv_width = wq.shape[2], wkv.shape[3]
    kv_block = min(2 * HD, kv_width)
    groups = kv_width // kv_block
    q_block = q_width // groups
    steps = 2
    depth = width // steps
    samples = n_done // (seq - seq // n_tp)
    block = seq // (n_dp * n_tp)
    packed = q_block + 2 * kv_block
    fixed = lambda g, k: (0, 0)
    in_specs = [pl.BlockSpec(p.shape, fixed, pipeline_mode=pl.Buffered(1)) for p in pieces] + [
        pl.BlockSpec((1, width), fixed),
        pl.BlockSpec((seq, HD), fixed),
        pl.BlockSpec((seq, HD), fixed),
        pl.BlockSpec((seq, seq), fixed),
        pl.BlockSpec((None, depth, q_block), lambda g, k: (0, k, g)),
        pl.BlockSpec((None, 2, depth, kv_block), lambda g, k: (0, 0, k, g)),
    ]
    operands = [*pieces, gain, cos, sin, mask, wq, wkv]
    out_shape, out_specs = [], []
    if prior is not None:
        operands.append(prior)
        in_specs.append(pl.BlockSpec((None, prior.shape[1], packed), lambda g, k: (g, 0, 0)))
        out_shape.append(jax.ShapeDtypeStruct((n_dp, n_tp, samples, block, q_width), jnp.bfloat16))
        out_specs.append(pl.BlockSpec((n_dp, n_tp, samples, block, q_block), lambda g, k: (0, 0, 0, 0, g)))
    if n_done < rows:
        out_shape.append(jax.ShapeDtypeStruct((groups, rows - n_done, packed), jnp.bfloat16))
        out_specs.append(pl.BlockSpec((None, rows - n_done, packed), lambda g, k: (g, 0, 0)))
    return pl.pallas_call(
        functools.partial(attention_kernel, n_dp, n_tp, len(pieces), n_done, prior is not None),
        out_shape=out_shape,
        grid=(groups, steps),
        in_specs=in_specs,
        out_specs=out_specs,
        scratch_shapes=[
            pltpu.VMEM((steps, rows, depth), jnp.bfloat16),
            pltpu.VMEM((rows, q_block), jnp.float32),
            pltpu.VMEM((rows, kv_block), jnp.float32),
            pltpu.VMEM((rows, kv_block), jnp.float32),
        ],
        compiler_params=params(),
        cost_estimate=pl.CostEstimate(flops=1, bytes_accessed=1, transcendentals=0),
        name="project_and_attend",
    )(*operands)


def out_kernel(ctx_ref, wo_ref, own_ref, send_ref):
    full = jnp.dot(ctx_ref[...], wo_ref[...], preferred_element_type=jnp.float32).astype(jnp.bfloat16)
    mine = own_ref.shape[0]
    own_ref[...] = full[:mine]
    send_ref[...] = full[mine:]


def out_projection(ctx, wo, mine, first, cols):
    rows, depth = ctx.shape
    col_block = min(512, cols)
    inner = cols // col_block
    base = first // col_block
    return pl.pallas_call(
        out_kernel,
        out_shape=[
            jax.ShapeDtypeStruct((mine, cols), jnp.bfloat16),
            jax.ShapeDtypeStruct((rows - mine, cols), jnp.bfloat16),
        ],
        grid=(inner,),
        in_specs=[
            pl.BlockSpec((rows, depth), lambda n: (0, 0)),
            pl.BlockSpec((None, depth, col_block), lambda n: (0, 0, base + n)),
        ],
        out_specs=[
            pl.BlockSpec((mine, col_block), lambda n: (0, n)),
            pl.BlockSpec((rows - mine, col_block), lambda n: (0, n)),
        ],
        compiler_params=params(),
        cost_estimate=pl.CostEstimate(flops=1, bytes_accessed=1, transcendentals=0),
        name="out_projection",
    )(ctx, wo)


def join_kernel(n_slots, block, table_ref, near_ref, far_ref, near_other, far_other, resid_ref, pair_ref, head_ref, *out_refs):
    packed_refs, stats_ref = out_refs[:-1], out_refs[-1]
    head = head_ref[...]
    lane = lax.broadcasted_iota(jnp.int32, (block, HD), 1)
    row = lax.broadcasted_iota(jnp.int32, (block, 1), 0)
    step = pl.program_id(0)
    slots = packed_refs[0].shape[0]

    for dest, packed_ref in enumerate(packed_refs):
        for slot in range(slots):
            entry = dest * n_slots + step * slots + slot
            part, resid, live = table_ref[0, entry], table_ref[1, entry], table_ref[2, entry]
            is_far = table_ref[4, entry] > 0
            added = jnp.where(is_far, far_ref[part], near_ref[part]).astype(jnp.float32)
            for k in range(near_other.shape[0]):
                added = added + jnp.where(is_far, far_other[k, part], near_other[k, part]).astype(jnp.float32)
            rows_in = jnp.where(table_ref[3, entry] > 0, pair_ref[resid], resid_ref[resid])
            hidden = rows_in.astype(jnp.float32) + added
            packed_ref[slot] = jnp.where(row < live, hidden, 0.0).astype(jnp.bfloat16)
            squares = jnp.sum(hidden * hidden, axis=-1, keepdims=True)
            scored = jnp.sum(hidden * head, axis=-1, keepdims=True)
            stats_ref[dest, slot] = jnp.where(lane == 0, squares, jnp.where(lane == 1, scored, 0.0))


def join(table, owns, others, resid, resid_pair, head, chunk, n_dp, n_slots, block):
    cols = owns[0][0].shape[-1]
    blocks = resid.shape[0]
    slots = n_slots // 2
    fixed = lambda i, t: (0, 0, 0)
    here = lambda i, t: (0, 0, chunk)
    out = pl.pallas_call(
        functools.partial(join_kernel, n_slots, block),
        out_shape=[jax.ShapeDtypeStruct((n_slots, block, cols), jnp.bfloat16) for _ in range(n_dp)]
        + [jax.ShapeDtypeStruct((n_dp, n_slots, block, HD), jnp.float32)],
        grid_spec=pltpu.PrefetchScalarGridSpec(
            num_scalar_prefetch=1,
            grid=(n_slots // slots,),
            in_specs=[
                *[pl.BlockSpec((blocks, block, cols), lambda i, t, at=at: (at, 0, 0)) for _, at in owns],
                *[pl.BlockSpec((v.shape[0], blocks, block, cols), lambda i, t, at=at: (0, at, 0, 0)) for v, at in others],
                pl.BlockSpec((resid.shape[0], block, cols), here),
                pl.BlockSpec((resid.shape[0], block, cols), here),
                pl.BlockSpec((1, cols), lambda i, t: (0, chunk)),
            ],
            out_specs=[pl.BlockSpec((slots, block, cols), lambda i, t: (i, 0, 0)) for _ in range(n_dp)]
            + [pl.BlockSpec((n_dp, slots, block, HD), lambda i, t: (0, i, 0, 0))],
        ),
        compiler_params=params(),
        cost_estimate=pl.CostEstimate(flops=1, bytes_accessed=1, transcendentals=0),
        name="join_partials",
    )(table, *[v for v, _ in owns], *[v for v, _ in others], resid, resid_pair, head)
    return list(out[:-1]), out[-1]


def place_kernel(count, order_ref, *refs):
    out_ref = refs[-1]
    for k in range(count):
        out_ref[:, order_ref[k]] = refs[k][...]


def place(order, pieces, whole, chunk, width):
    n_slots, block, cols = pieces[0].shape
    count = len(pieces)
    rows = n_slots // 3
    specs = [pl.BlockSpec((rows, block, cols), lambda i, o: (i, 0, 0)) for _ in pieces]
    operands = list(pieces)
    aliases = {}
    if whole is not None:
        specs.append(pl.BlockSpec(memory_space=pl.ANY))
        operands.append(whole)
        aliases = {1 + count: 0}
    return pl.pallas_call(
        functools.partial(place_kernel, count),
        out_shape=jax.ShapeDtypeStruct((n_slots, count, block, width), jnp.bfloat16),
        grid_spec=pltpu.PrefetchScalarGridSpec(
            num_scalar_prefetch=1,
            grid=(n_slots // rows,),
            in_specs=specs,
            out_specs=pl.BlockSpec((rows, count, block, cols), lambda i, o: (i, 0, 0, chunk)),
        ),
        input_output_aliases=aliases,
        compiler_params=params(),
        cost_estimate=pl.CostEstimate(flops=1, bytes_accessed=1, transcendentals=0),
        name="place_rows",
    )(order, *operands)


def on_device(responses, lengths, dest_dp, dest_slot, wq, wkv, wo, norm_gain, head_vec):
    n_sec = lax.axis_size("sec")
    n_dp = lax.axis_size("dp")
    n_tp = lax.axis_size("tp")
    _, local_len, width = responses.shape
    samples = lengths.shape[0]
    n_slots = 3 * samples // (2 * n_dp)
    seq = local_len * n_tp
    block = local_len // n_dp
    my_sec, my_dp, my_tp = lax.axis_index("sec"), lax.axis_index("dp"), lax.axis_index("tp")

    owners = lax.rem(my_tp - jnp.arange(n_tp) + n_tp, n_tp)
    positions = (owners[:, None] * local_len + jnp.arange(local_len)[None, :]).reshape(seq)
    frequency = jnp.exp(jnp.arange(HD // 2, dtype=jnp.float32) * (-2.0 * math.log(ROPE_THETA) / HD))
    angles = positions.astype(jnp.float32)[:, None] * frequency[None, :]
    cos = jnp.tile(jnp.cos(angles), (1, 2))
    sin = jnp.concatenate([-jnp.sin(angles), jnp.sin(angles)], axis=1)
    mask = (positions[:, None] >= positions[None, :]).astype(jnp.float32)

    attend = lambda pieces, prior, n_done: attention(
        pieces, prior, n_done, norm_gain, cos, sin, mask, wq, wkv, n_dp, n_tp
    )

    def by_step(ctx):
        return [lax.dynamic_index_in_dim(ctx, my_dp ^ k, 0, keepdims=False) for k in range(n_dp)]

    def spread(parts):
        return [parts[0]] + [swap(parts[k], "dp", n_dp, k) for k in range(1, n_dp)]

    def gathered(parts):
        return jnp.stack(parts, axis=1).reshape(-1, wq.shape[2])

    mine = responses[0]
    near = [shift(mine, "tp", n_tp, k) for k in range(1, n_tp)]
    far_mine = swap(mine, "sec", n_sec, 2)
    mine_pair = swap(mine, "sec", n_sec, 1)
    mine, mine_pair, cos, sin, mask = sync((mine, mine_pair, cos, sin, mask))
    quarter = lambda k: lax.dynamic_slice_in_dim(mine, (my_dp ^ k) * block, block, 0)
    resid = [quarter(0)] + [swap(quarter(k), "dp", n_dp, k) for k in range(1, n_dp)]
    (kept,) = attend([mine, mine_pair], None, 0)
    near, far_mine, resid, kept = sync((near, far_mine, resid, kept))

    far = [shift(far_mine, "tp", n_tp, k) for k in range(1, n_tp)]
    near_pair = [swap(v, "sec", n_sec, 1) for v in near]
    far_mine_pair = swap(far_mine, "sec", n_sec, 1)
    resid = jnp.stack(resid)
    resid_far = swap(resid, "sec", n_sec, 2)
    near, near_pair, far_mine, far_mine_pair, kept = sync((near, near_pair, far_mine, far_mine_pair, kept))

    more = 2 * (seq - local_len)
    near_ctx, kept = attend(near + near_pair + [far_mine, far_mine_pair], kept, more)
    near_ctx, kept, far, resid, resid_far = sync((near_ctx, kept, far, resid, resid_far))

    near_rows = spread(by_step(near_ctx))
    far_pair = [swap(v, "sec", n_sec, 1) for v in far]
    far, far_pair, kept = sync((far, far_pair, kept))
    (far_ctx,) = attend(far + far_pair, kept, more)
    across = lax.dynamic_index_in_dim(far_ctx, my_dp ^ 2, 0, keepdims=False)
    near_rows, far_ctx, across = sync((near_rows, far_ctx, across))

    row_dp = lax.dynamic_index_in_dim(dest_dp, my_sec, 0, keepdims=False)
    row_slot = lax.dynamic_index_in_dim(dest_slot, my_sec, 0, keepdims=False)
    sample = jnp.arange(samples)
    i_rel = my_sec ^ (sample // n_dp)
    k_rel = my_dp ^ (sample % n_dp)
    part_at = k_rel * 2 + i_rel % 2
    resid_at = (i_rel // 2) * n_dp + k_rel
    dests = my_dp ^ jnp.arange(n_dp)
    chosen = (row_dp[None, None, :] == dests[:, None, None]) & (
        row_slot[None, None, :] == jnp.arange(n_slots)[None, :, None]
    )
    first_pos = my_tp * local_len + my_dp * block
    live = jnp.clip(lengths - first_pos, 0, block)
    pick = lambda v: jnp.sum(jnp.where(chosen, v[None, None, :], 0), axis=-1).reshape(-1)
    table = jnp.stack([pick(part_at), pick(resid_at), pick(live), pick(i_rel % 2), pick(i_rel // 2)]).astype(jnp.int32)
    order = dests.astype(jnp.int32)

    unit = width // sum(CHUNKS)
    starts = [unit * sum(CHUNKS[:c]) for c in range(len(CHUNKS))]
    count = len(CHUNKS)

    def project(chunk, ctx_rows):
        owned = ctx_rows.shape[0] // n_tp
        own, send = out_projection(ctx_rows, wo, owned, starts[chunk], unit * CHUNKS[chunk])
        own = own.reshape(-1, block, own.shape[-1])
        return own, send.reshape(n_tp - 1, -1, block, own.shape[-1])

    def exchange(projected):
        send = projected[1]
        return jnp.stack([shift(send[k - 1], "tp", n_tp, n_tp - k) for k in range(1, n_tp)])

    def finish(chunk, owns, others):
        return join(
            table, owns, others, resid, resid_pair, head_vec, starts[chunk] // (unit * CHUNKS[chunk]),
            n_dp, n_slots, block,
        )

    def put(whole, chunk, pieces):
        return place(order, pieces, whole, starts[chunk] // (unit * CHUNKS[chunk]), width)

    far_across = swap(across, "dp", n_dp, 2)
    far_rows, near_rows = by_step(far_ctx), gathered(near_rows)
    resid = jnp.concatenate([resid, resid_far], axis=0)
    far_rows, near_rows, resid = sync((far_rows, near_rows, resid))
    near_projected = [project(c, near_rows) for c in range(2)]
    far_rows, far_across, near_projected, near_rows, resid = sync(
        (far_rows, far_across, near_projected, near_rows, resid)
    )
    far_rows = [far_across if k == 2 else swap(v, "dp", n_dp, k) if k else v for k, v in enumerate(far_rows)]
    near_others = [exchange(p) for p in near_projected]
    resid_pair = swap(resid, "sec", n_sec, 1)
    near_projected += [project(c, near_rows) for c in range(2, SPLIT)]
    far_rows, near_others, near_projected, near_rows, resid_pair = sync(
        (far_rows, near_others, near_projected, near_rows, resid_pair)
    )

    far_rows = gathered(far_rows)
    far_projected = [project(0, far_rows)]
    far_projected, far_rows = sync((far_projected, far_rows))
    far_others = [exchange(far_projected[0])]
    far_projected.append(project(1, far_rows))
    far_others, far_projected, far_rows = sync((far_others, far_projected, far_rows))

    def halves(near, far):
        return [(near, 0), (far, 0)]

    packed, part = finish(
        0, halves(near_projected[0][0], far_projected[0][0]), halves(near_others[0], far_others[0])
    )
    packed, far_projected, far_rows = sync((packed, far_projected, far_rows))

    stats, whole, pieces, projected = [part], None, None, None
    all_rows = jnp.concatenate([v.reshape(n_tp, -1, v.shape[-1]) for v in (near_rows, far_rows)], axis=1)
    all_rows = all_rows.reshape(-1, wq.shape[2])
    for chunk in range(count):
        moved = [packed[0]] + [swap(packed[k], "dp", n_dp, k) for k in range(1, n_dp)]
        if pieces is not None:
            whole = put(whole, chunk - 1, pieces)
        ahead = chunk + 1
        if ahead < count:
            if ahead < SPLIT:
                owns = halves(near_projected[ahead][0], far_projected[ahead][0])
                others = halves(near_others[ahead], exchange(far_projected[ahead]))
            else:
                other = exchange(projected)
                owns, others = [(projected[0], 0), (projected[0], 1)], [(other, 0), (other, 1)]
            if ahead + 1 < SPLIT:
                near_others.append(exchange(near_projected[ahead + 1]))
                far_projected.append(project(ahead + 1, far_rows))
            elif ahead + 1 < count:
                projected = project(ahead + 1, all_rows)
            packed, part = finish(ahead, owns, others)
            stats.append(part)
            moved, packed, whole, all_rows, far_projected, near_others, projected = sync(
                (moved, packed, whole, all_rows, far_projected, near_others, projected)
            )
        pieces = moved
    whole = put(whole, count - 1, pieces)
    layer_out = jnp.transpose(whole.reshape(n_slots, local_len, width), (1, 0, 2))[None, None]

    stats = sum(v[..., :2] for v in stats)
    token_scores = stats[..., 1] * lax.rsqrt(stats[..., 0] * (1.0 / width) + NORM_EPS)
    is_live = jnp.arange(block)[None, None, :] < table[2].reshape(n_dp, n_slots, 1)
    slot_sums = jnp.sum(jnp.where(is_live, token_scores, 0.0), axis=-1)
    by_sample = jnp.sum(jnp.where(chosen, slot_sums[:, :, None], 0.0), axis=(0, 1))
    by_model = jnp.where(jnp.arange(n_sec)[:, None] == my_sec, by_sample[None, :], 0.0)
    for axis, size in (("tp", n_tp), ("dp", n_dp), ("sec", n_sec)):
        by_model = sum([shift(by_model, axis, size, k) for k in range(1, size)], by_model)
    totals = by_model
    averages = totals / lengths[None, :].astype(jnp.float32)
    owner = (dest_dp[n_sec - 1] == my_dp)[None, :] & (
        dest_slot[n_sec - 1][None, :] == jnp.arange(n_slots)[:, None]
    )
    sample_scores = jnp.sum(jnp.where(owner[:, None, :], averages[None, :, :], 0.0), axis=-1)
    return layer_out, sample_scores[None]


def solution(mesh):
    placed = (
        P(("sec", "dp"), "tp", None),
        P(),
        P(),
        P(),
        P("sec", None, "tp"),
        P("sec", None, None, "tp"),
        P("sec", "tp", None),
        P("sec", None),
        P("sec", None),
    )
    return jax.shard_map(
        on_device,
        mesh=mesh,
        in_specs=placed,
        out_specs=(P("sec", "dp", "tp", None, None), P("dp", None, None)),
        check_vma=False,
    )
```
